32 devices in a mesh: dp: 4 (over y, core), expert: 8 (over z, x).
Axes of the slice: x: 2, y: 2, z: 4, core: 2. Of those that a mesh axis runs over, the one named last changes fastest.
Arguments:
- tokens: bfloat16 [512, 3584], P('expert', 'dp'), may hold values from -6 to 6
- expert_ids: int32 [512, 8], P('expert'), may hold values from 0 to 31, as said below
- gate_weights: float32 [512, 8], P('expert'), may hold values from 0.1 to 1
- w_gate: bfloat16 [32, 3584, 1024], P('expert', 'dp'), may hold values from -0.09375 to 0.09375
- w_up: bfloat16 [32, 3584, 1024], P('expert', 'dp'), may hold values from -0.09375 to 0.09375
- w_down: bfloat16 [32, 1024, 3584], P('expert', None, 'dp'), may hold values from -0.1875 to 0.1875
- cotangent: bfloat16 [512, 3584], P('expert', 'dp'), may hold values from -6 to 6
Outputs:
- mixed: bfloat16 [512, 3584], P('expert', 'dp')
- token_grad: bfloat16 [512, 3584], P('expert', 'dp')
- grad_gate: bfloat16 [32, 3584, 1024], P('expert', 'dp')
- grad_up: bfloat16 [32, 3584, 1024], P('expert', 'dp')
- grad_down: bfloat16 [32, 1024, 3584], P('expert', None, 'dp')
The draws below stay inside these ranges and needn't reach their ends.
Inputs may be any that keep to these rules, and one draw needn't show every extreme that they name: `expert_ids`: each row names 8 different experts. In each aligned block of 64 rows (the rows of one device) no expert is named by more than 32 rows, and one expert, the same in every block, is named by exactly 32 rows of every block.
All inputs are finite; a program needn't handle non-finite values.
Results may differ from the reference program's by a relative error of at most 0.035.
Values may be sent and summed in bfloat16 or wider, within the bound.
A program may use at most 128 MiB of HBM per device.

```python
import math
import jax
import jax.numpy as jnp
from jax import lax

D = 3584
FFW = 1024
EXPERTS = 32
TOPK = 8
TOK_DEV = 64
CAP = 32
TOKENS = 512
N_DP = 4


def pick_from(order, position):
    return order[position]


def draw_expert_ids(key, part):
    key = jax.random.fold_in(key, 11)
    hot_key, order_key, shift_key, phase_key = jax.random.split(key, 4)
    blocks = TOKENS // TOK_DEV
    others = EXPERTS - 1
    hot_expert = jax.random.randint(hot_key, (), 0, EXPERTS)
    orders = jax.vmap(lambda block_key: jax.random.permutation(block_key, others))(jax.random.split(order_key, blocks))
    orders = (orders + (orders >= hot_expert).astype(jnp.int32)).astype(jnp.int32)
    shifts = jax.random.randint(shift_key, (blocks, 1), 0, TOK_DEV)
    phases = jax.random.randint(phase_key, (blocks, 1), 0, others)
    row_numbers = jnp.arange(TOK_DEV, dtype=jnp.int32)[None, :]
    has_hot = ((row_numbers + shifts) % TOK_DEV < CAP).astype(jnp.int32)
    window_start = (TOPK * row_numbers + phases) % others
    choice_numbers = jnp.arange(TOPK, dtype=jnp.int32)[None, None, :]
    position = (window_start[:, :, None] + choice_numbers - has_hot[:, :, None]) % others
    chosen = jax.vmap(pick_from)(orders, position)
    picked = jnp.where((choice_numbers == 0) & (has_hot[:, :, None] == 1), hot_expert, chosen)
    return picked.reshape(TOKENS, TOPK).astype(jnp.int32)


def block_scale(rng, extent, cuts, low, largest):
    level, own = 1.0, jax.random.fold_in(rng, 6)
    for dim, blocks in cuts:
        steps = jnp.exp(jax.random.uniform(jax.random.fold_in(own, dim), (blocks,), jnp.float32, low / len(cuts), largest / len(cuts)))
        level = level * jnp.repeat(steps, extent[dim] // blocks).reshape([-1 if axis == dim else 1 for axis in range(len(extent))])
    return level


def scatter_about(rng, dims, deviation, most, shards=(), held_as=jnp.bfloat16):
    array = jax.random.normal(rng, dims, jnp.float32) * deviation
    if len(shards) > 0:
        array = block_scale(rng, dims, shards, -0.22, 0.18) * array
    return jnp.clip(array, min=-most, max=most).astype(held_as)


def setup_inputs(seed: int = 0) -> dict:
    arg_keys = jax.random.split(jax.random.key(seed), 8)
    return {
        "tokens": scatter_about(arg_keys[0], (TOKENS, D), 1.0, 6.0, ((0, 8), (1, 4))),
        "expert_ids": draw_expert_ids(jax.random.fold_in(arg_keys[7], 71), 0),
        "gate_weights": jnp.clip(jnp.exp(math.log(1.0) - 2.3025851 * jax.random.uniform(arg_keys[2], (TOKENS, TOPK), jnp.float32) ** block_scale(arg_keys[2], (TOKENS, TOPK), ((0, 8),), -0.2, 0.2)), 0.1, 1.0),
        "w_gate": scatter_about(arg_keys[3], (EXPERTS, D, FFW), D ** -0.5, 0.09375, ((0, 8), (1, 4))),
        "w_up": scatter_about(arg_keys[4], (EXPERTS, D, FFW), D ** -0.5, 0.09375, ((0, 8), (1, 4))),
        "w_down": scatter_about(arg_keys[5], (EXPERTS, FFW, D), FFW ** -0.5, 0.1875, ((0, 8), (2, 4))),
        "cotangent": scatter_about(arg_keys[6], (TOKENS, D), 1.0, 6.0, ((0, 8), (1, 4))),
    }


def slot_pairs(expert_ids):
    blocks = TOKENS // TOK_DEV
    pair_count = TOK_DEV * TOPK
    flat_ids = expert_ids.reshape(blocks, pair_count).astype(jnp.int32)
    numbers = jnp.arange(EXPERTS, dtype=jnp.int32)
    onehot = (flat_ids[:, :, None] == numbers[None, None, :]).astype(jnp.int32)
    slot_rank = jnp.sum((jnp.cumsum(onehot, axis=1) - 1) * onehot, axis=2).astype(jnp.int32)
    block_index = jnp.broadcast_to(jnp.arange(blocks, dtype=jnp.int32)[:, None], (blocks, pair_count))
    pair_index = (jnp.arange(pair_count, dtype=jnp.int32)[None, :] + block_index * pair_count).astype(jnp.int32)
    table = jnp.full((EXPERTS, blocks, CAP), TOKENS * TOPK, dtype=jnp.int32)
    table = table.at[flat_ids, block_index, slot_rank].set(pair_index)
    return table.reshape(EXPERTS, blocks * CAP)


def block_product(left, right):
    rows = left.shape[0]
    cols = right.shape[1]
    left_blocks = left.astype(jnp.float32).reshape(rows, N_DP, D // N_DP)
    right_blocks = right.astype(jnp.float32).reshape(N_DP, D // N_DP, cols)
    partial_sums = jnp.einsum("rbd,bdf->brf", left_blocks, right_blocks, precision=lax.Precision.HIGHEST)
    rounded = lax.optimization_barrier(partial_sums.astype(jnp.bfloat16))
    return jnp.sum(rounded.astype(jnp.float32), axis=0)


def expert_pass(inputs):
    rows_in, rows_dy, gate_matrix, up_matrix, down_matrix = inputs
    gate_sum = block_product(rows_in, gate_matrix)
    up_sum = block_product(rows_in, up_matrix)
    logistic = jax.nn.sigmoid(gate_sum)
    hidden = (gate_sum * logistic * up_sum).astype(jnp.bfloat16)
    expert_out = jnp.dot(hidden, down_matrix, preferred_element_type=jnp.float32).astype(jnp.bfloat16)
    hidden_grad = block_product(rows_dy, down_matrix.T)
    up_grad = (hidden_grad * gate_sum * logistic).astype(jnp.bfloat16)
    gate_grad = (hidden_grad * up_sum * logistic * (1.0 + gate_sum * (1.0 - logistic))).astype(jnp.bfloat16)
    row_grad = (jnp.dot(gate_grad, gate_matrix.T, preferred_element_type=jnp.float32)
                + jnp.dot(up_grad, up_matrix.T, preferred_element_type=jnp.float32)).astype(jnp.bfloat16)
    grad_gate = jnp.dot(rows_in.T, gate_grad, preferred_element_type=jnp.float32).astype(jnp.bfloat16)
    grad_up = jnp.dot(rows_in.T, up_grad, preferred_element_type=jnp.float32).astype(jnp.bfloat16)
    grad_down = jnp.dot(hidden.T, rows_dy, preferred_element_type=jnp.float32).astype(jnp.bfloat16)
    return expert_out, row_grad, grad_gate, grad_up, grad_down


def reference(tokens, expert_ids, gate_weights, w_gate, w_up, w_down, cotangent):
    pairs = slot_pairs(expert_ids)
    token_of = (pairs // TOPK).astype(jnp.int32)
    gates_padded = jnp.concatenate([gate_weights.reshape(-1), jnp.zeros((1,), jnp.float32)])
    pair_gates = gates_padded[pairs]
    tokens_padded = jnp.concatenate([tokens, jnp.zeros((1, D), jnp.bfloat16)], axis=0)
    cot_padded = jnp.concatenate([cotangent, jnp.zeros((1, D), jnp.bfloat16)], axis=0)
    rows_in = tokens_padded[token_of]
    rows_dy = (pair_gates[:, :, None] * cot_padded[token_of].astype(jnp.float32)).astype(jnp.bfloat16)
    expert_out, row_grad, grad_gate, grad_up, grad_down = lax.map(
        expert_pass, (rows_in, rows_dy, w_gate, w_up, w_down))
    mixed = jnp.zeros((TOKENS + 1, D), jnp.float32).at[token_of].add(
        pair_gates[:, :, None] * expert_out.astype(jnp.float32))
    token_grad = jnp.zeros((TOKENS + 1, D), jnp.float32).at[token_of].add(row_grad.astype(jnp.float32))
    return (mixed[:TOKENS].astype(jnp.bfloat16), token_grad[:TOKENS].astype(jnp.bfloat16),
            grad_gate, grad_up, grad_down)
```

```python
import jax
import jax.numpy as jnp
from jax import lax
from jax.sharding import PartitionSpec as P

EXPERTS = 32
CAP = 32
F32 = jnp.float32
BF16 = jnp.bfloat16


def mm(a, b, dims=((1,), (0,))):
    return lax.dot_general(a, b, (dims, ((), ())), preferred_element_type=F32)


def tables(ids_all, gates_all, first_expert, local_count, blocks):
    tok = ids_all.shape[0] // blocks
    mine = first_expert + jnp.arange(local_count, dtype=jnp.int32)
    hits = ids_all[None, :, :] == mine[:, None, None]
    named = jnp.any(hits, axis=2).reshape(local_count, blocks, tok)
    gate = jnp.sum(jnp.where(hits, gates_all[None], 0.0), axis=2).reshape(local_count, blocks, tok)
    earlier = jnp.triu(jnp.ones((tok, tok), BF16), 1)
    rank = jnp.einsum("ebs,st->ebt", named.astype(BF16), earlier, preferred_element_type=F32)
    slot = jnp.arange(CAP, dtype=jnp.int32)
    block = jnp.arange(blocks, dtype=jnp.int32)
    where = jnp.where(named, rank.astype(jnp.int32), -1)
    pick = (where[:, None, None, :, :] == slot[None, None, :, None, None]) & (
        block[None, :, None, None, None] == block[None, None, None, :, None]
    )
    shape = (local_count * blocks * CAP, blocks * tok)
    weighted = jnp.where(pick, gate[:, None, None, :, :], 0.0)
    row_gate = jnp.sum(weighted, axis=(3, 4)).reshape(-1, 1)
    return pick.astype(BF16).reshape(shape), weighted.astype(BF16).reshape(shape), row_gate


def send(x, axis, pairs):
    return lax.ppermute(x, axis, pairs)


def flip(size, bit):
    return [(i, i ^ bit) for i in range(size)]


def at(x, i):
    return lax.dynamic_index_in_dim(x, i, 0, keepdims=False)


def dp_sum_pair(part, core, n_dp):
    got = send(at(part, 1 - core), "dp", flip(n_dp, 1))
    both = (at(part, core).astype(F32) + got.astype(F32)).astype(BF16)
    far = send(both, "dp", flip(n_dp, 2))
    return both.astype(F32) + far.astype(F32)


def share_pair(x, core, n_dp):
    got = send(x, "dp", flip(n_dp, 1))
    return jnp.where(core == 0, jnp.stack([x, got]), jnp.stack([got, x]))


def return_sum(full, n_ex):
    tok = full.shape[0] // n_ex
    n_z = n_ex // 2
    me = lax.axis_index("expert")
    z, x = me // 2, me % 2
    parts = full.reshape(n_z, 2, tok, full.shape[1])
    got = send(lax.dynamic_index_in_dim(parts, 1 - x, 1, keepdims=False), "expert", flip(n_ex, 1))
    keep = lax.dynamic_index_in_dim(parts, x, 1, keepdims=False)
    col = (keep.astype(F32) + got.astype(F32)).astype(BF16)
    total = at(col, z).astype(F32)
    for k in range(1, n_z):
        to = [(i, (i + 2 * k) % n_ex) for i in range(n_ex)]
        total += send(at(col, (z + k) % n_z), "expert", to).astype(F32)
    return total.astype(BF16)


def make_body(n_dp, n_ex):
    fast = n_dp == 4 and n_ex == 8

    def body(tokens, expert_ids, gate_weights, w_gate, w_up, w_down, cotangent):
        width = tokens.shape[1]
        count = w_gate.shape[0]
        rows = n_ex * CAP
        core = lax.axis_index("dp") % 2
        route = jnp.concatenate([expert_ids.astype(F32), gate_weights], axis=1)
        route = lax.all_gather(route, "expert", axis=0, tiled=True)
        top = expert_ids.shape[1]
        both = jnp.concatenate([tokens, cotangent], axis=1)
        both = lax.all_gather(both, "expert", axis=0, tiled=True)
        pick, weighted, row_gate = tables(
            route[:, :top].astype(jnp.int32),
            route[:, top:],
            lax.axis_index("expert") * count,
            count,
            n_ex,
        )
        picked = mm(pick, both)
        rows_in = picked[:, :width].astype(BF16).reshape(count, rows, width)
        rows_dy = (picked[:, width:] * row_gate).astype(BF16).reshape(count, rows, width)

        def gate_up(e, w):
            return mm(rows_in[e], w[e]).astype(BF16)

        def back(e):
            return mm(rows_dy[e], w_down[e], ((1,), (1,))).astype(BF16)

        def forward(gate_sum, up_sum):
            logistic = jax.nn.sigmoid(gate_sum)
            return (gate_sum * logistic * up_sum).astype(BF16)

        def backward(gate_sum, up_sum, hidden_grad):
            logistic = jax.nn.sigmoid(gate_sum)
            up_grad = (hidden_grad * gate_sum * logistic).astype(BF16)
            gate_grad = (
                hidden_grad * up_sum * logistic * (1.0 + gate_sum * (1.0 - logistic))
            ).astype(BF16)
            return gate_grad, up_grad

        if fast:
            halves = range(0, count, 2)
            sums = []
            for e in halves:
                g = dp_sum_pair(jnp.stack([gate_up(e, w_gate), gate_up(e + 1, w_gate)]), core, n_dp)
                u = dp_sum_pair(jnp.stack([gate_up(e, w_up), gate_up(e + 1, w_up)]), core, n_dp)
                sums.append((g, u))
            grads = [dp_sum_pair(jnp.stack([back(e), back(e + 1)]), core, n_dp) for e in halves]
            hidden = jnp.concatenate([share_pair(forward(g, u), core, n_dp) for g, u in sums])
            pairs = [
                share_pair(jnp.stack(backward(g, u, h)), core, n_dp)
                for (g, u), h in zip(sums, grads)
            ]
            gate_grad = jnp.concatenate([p[:, 0] for p in pairs])
            up_grad = jnp.concatenate([p[:, 1] for p in pairs])
        else:
            gate_sum, up_sum, hidden_grad = (
                lax.psum(jnp.stack(p), "dp").astype(F32)
                for p in (
                    [gate_up(e, w_gate) for e in range(count)],
                    [gate_up(e, w_up) for e in range(count)],
                    [back(e) for e in range(count)],
                )
            )
            hidden = forward(gate_sum, up_sum)
            gate_grad, up_grad = backward(gate_sum, up_sum, hidden_grad)

        out_rows = jnp.concatenate([mm(hidden[e], w_down[e]).astype(BF16) for e in range(count)])
        mixed = mm(weighted, out_rows, ((0,), (0,))).astype(BF16)
        row_grad = jnp.concatenate(
            [
                (
                    mm(gate_grad[e], w_gate[e], ((1,), (1,))) + mm(up_grad[e], w_up[e], ((1,), (1,)))
                ).astype(BF16)
                for e in range(count)
            ]
        )
        token_grad = mm(pick, row_grad, ((0,), (0,))).astype(BF16)
        if fast:
            mixed, token_grad = return_sum(mixed, n_ex), return_sum(token_grad, n_ex)
        else:
            mixed, token_grad = (
                lax.psum_scatter(v, "expert", scatter_dimension=0, tiled=True)
                for v in (mixed, token_grad)
            )
        grad_gate = jnp.einsum(
            "erd,erf->edf", rows_in, gate_grad, preferred_element_type=F32
        ).astype(BF16)
        grad_up = jnp.einsum(
            "erd,erf->edf", rows_in, up_grad, preferred_element_type=F32
        ).astype(BF16)
        grad_down = jnp.einsum(
            "erf,erd->efd", hidden, rows_dy, preferred_element_type=F32
        ).astype(BF16)
        return mixed, token_grad, grad_gate, grad_up, grad_down

    return body


def solution(mesh):
    placed = (
        P("expert", "dp"),
        P("expert", None),
        P("expert", None),
        P("expert", "dp", None),
        P("expert", "dp", None),
        P("expert", None, "dp"),
        P("expert", "dp"),
    )
    return jax.shard_map(
        make_body(mesh.shape["dp"], mesh.shape["expert"]),
        mesh=mesh,
        in_specs=placed,
        out_specs=(
            P("expert", "dp"),
            P("expert", "dp"),
            P("expert", "dp", None),
            P("expert", "dp", None),
            P("expert", None, "dp"),
        ),
        check_vma=False,
    )
```

```python
import jax
import jax.numpy as jnp
from jax import lax
from jax.experimental import pallas as pl
from jax.experimental.pallas import tpu as pltpu
from jax.sharding import PartitionSpec as P

EXPERTS = 32
CAP = 32
F32 = jnp.float32
BF16 = jnp.bfloat16


def mm(a, b, dims=((1,), (0,))):
    return lax.dot_general(a, b, (dims, ((), ())), preferred_element_type=F32)


def tables(ids_all, gates_all, first_expert, local_count, blocks):
    tok = ids_all.shape[0] // blocks
    mine = first_expert + jnp.arange(local_count, dtype=jnp.int32)
    hits = ids_all[None, :, :] == mine[:, None, None]
    named = jnp.any(hits, axis=2).reshape(local_count, blocks, tok)
    gate = jnp.sum(jnp.where(hits, gates_all[None], 0.0), axis=2).reshape(local_count, blocks, tok)
    earlier = jnp.triu(jnp.ones((tok, tok), BF16), 1)
    rank = jnp.einsum("ebs,st->ebt", named.astype(BF16), earlier, preferred_element_type=F32)
    slot = jnp.arange(CAP, dtype=jnp.int32)
    block = jnp.arange(blocks, dtype=jnp.int32)
    where = jnp.where(named, rank.astype(jnp.int32), -1)
    pick = (where[:, None, None, :, :] == slot[None, None, :, None, None]) & (
        block[None, :, None, None, None] == block[None, None, None, :, None]
    )
    shape = (local_count * blocks * CAP, blocks * tok)
    weighted = jnp.where(pick, gate[:, None, None, :, :], 0.0)
    row_gate = jnp.sum(weighted, axis=(3, 4)).reshape(-1, 1)
    return pick.astype(BF16).reshape(shape), weighted.astype(BF16).reshape(shape), row_gate


def send(x, axis, pairs):
    return lax.ppermute(x, axis, pairs)


def flip(size, bit):
    return [(i, i ^ bit) for i in range(size)]


def at(x, i):
    return lax.dynamic_index_in_dim(x, i, 0, keepdims=False)


def return_sum(full, n_ex):
    tok = full.shape[0] // n_ex
    n_z = n_ex // 2
    me = lax.axis_index("expert")
    z, x = me // 2, me % 2
    parts = full.reshape(n_z, 2, tok, full.shape[1])
    got = send(lax.dynamic_index_in_dim(parts, 1 - x, 1, keepdims=False), "expert", flip(n_ex, 1))
    keep = lax.dynamic_index_in_dim(parts, x, 1, keepdims=False)
    col = (keep.astype(F32) + got.astype(F32)).astype(BF16)
    total = at(col, z).astype(F32)
    for k in range(1, n_z):
        to = [(i, (i + 2 * k) % n_ex) for i in range(n_ex)]
        total += send(at(col, (z + k) % n_z), "expert", to).astype(F32)
    return total.astype(BF16)


TILE = 256


def block_tables(route, first_expert, local_count, top):
    tok = route.shape[1]
    rows = local_count * CAP
    number = lax.broadcasted_iota(jnp.int32, (rows, tok), 0)
    wanted = (first_expert + number // CAP).astype(F32)
    named = jnp.zeros((rows, tok), F32)
    gate = jnp.zeros((rows, tok), F32)
    for k in range(top):
        hit = route[k : k + 1, :] == wanted
        named = jnp.where(hit, 1.0, named)
        gate = jnp.where(hit, route[top + k : top + k + 1, :], gate)
    before = lax.broadcasted_iota(jnp.int32, (tok, tok), 0)
    after = lax.broadcasted_iota(jnp.int32, (tok, tok), 1)
    earlier = jnp.where(before < after, 1.0, 0.0).astype(BF16)
    rank = jnp.dot(named.astype(BF16), earlier, preferred_element_type=F32)
    pick = jnp.where(rank == (number % CAP).astype(F32), named, 0.0)
    return pick, pick * gate


def front_kernel(
    both_ref, route_ref, wg_hbm, wu_hbm, wd_hbm,
    rows_in_out, rows_dy_out, pick_out, weighted_out, hidden_out, gate_grad_out, up_grad_out,
    wg, wu, wd, gathered, routes, rows_in, rows_dy, pick_all, weighted_all,
    away, own, near, far, hidden, gate_grad, up_grad,
    load_sem, keep_sem, tok_send, tok_recv, route_send, route_recv,
    core_send, core_recv, y_send, y_recv, share_send, share_recv, share_keep,
):
    count, width, ffw = wg.shape
    n_ex, tok, _ = gathered.shape
    n_z = n_ex // 2
    top = route_ref.shape[0] // 2
    dp = lax.axis_index("dp")
    me = lax.axis_index("expert")
    z = me // 2
    x = me % 2
    core = dp % 2
    x_peer = (dp, z * 2 + 1 - x)
    core_peer = (dp + 1 - 2 * core, me)
    y_peer = ((dp + 2) % 4, me)
    z_peers = [(dp, ((z + k) % n_z) * 2 + x) for k in range(1, n_z)]
    first_expert = me * count

    loads = [
        pltpu.make_async_copy(a, b, load_sem.at[i])
        for i, (a, b) in enumerate(((wg_hbm, wg), (wu_hbm, wu), (wd_hbm, wd)))
    ]
    for c in loads:
        c.start()

    barrier = pltpu.get_barrier_semaphore()
    peers = [x_peer, core_peer, y_peer] + z_peers
    for p in peers:
        pl.semaphore_signal(barrier, inc=1, device_id=p, device_id_type=pl.DeviceIdType.MESH)
    pl.semaphore_wait(barrier, len(peers))

    def remote(src, dst, s, r, i, to):
        return pltpu.make_async_remote_copy(
            src_ref=src, dst_ref=dst, send_sem=s.at[i], recv_sem=r.at[i],
            device_id=to, device_id_type=pl.DeviceIdType.MESH,
        )

    copies = {}
    for name, src, dst, s, r in (
        ("route", route_ref, routes, route_send, route_recv),
        ("tok", both_ref, gathered, tok_send, tok_recv),
    ):
        for k in range(1, n_z):
            copies[name, k] = remote(src, dst.at[me], s, r, k, z_peers[k - 1])
        copies[name, n_z] = remote(src, dst.at[me], s, r, n_z, x_peer)
        for k in range(1, n_z + 1):
            copies[name, k].start()

    gathered[me] = both_ref[...]
    routes[me] = route_ref[...]

    def place(b):
        pick, weighted = block_tables(routes[b], first_expert, count, top)
        row_gate = jnp.sum(weighted, axis=1, keepdims=True)
        sel = pick.astype(BF16)
        at = pl.ds(pl.multiple_of(b * CAP, CAP), CAP)
        a = jnp.dot(sel, gathered[b, :, :width], preferred_element_type=F32).astype(BF16)
        d = jnp.dot(sel, gathered[b, :, width:], preferred_element_type=F32) * row_gate
        d = d.astype(BF16)
        for e in range(count):
            rows_in[e, at, :] = a[e * CAP : (e + 1) * CAP]
            rows_dy[e, at, :] = d[e * CAP : (e + 1) * CAP]

    place(me)
    for k in range(1, n_z):
        slot = ((z + n_z - k) % n_z) * 2 + x
        for name, buf, s, r in (
            ("route", routes, route_send, route_recv),
            ("tok", gathered, tok_send, tok_recv),
        ):
            copies[name, k].wait_recv()
            copies[name, n_z + k] = remote(buf.at[slot], buf.at[slot], s, r, n_z + k, x_peer)
            copies[name, n_z + k].start()
        place(slot)
    for k in range(n_z):
        copies["route", n_z + k].wait_recv()
        copies["tok", n_z + k].wait_recv()
        place(((z + n_z - k) % n_z) * 2 + 1 - x)

    keeps = [
        pltpu.make_async_copy(rows_in, rows_in_out, keep_sem.at[0]),
        pltpu.make_async_copy(rows_dy, rows_dy_out, keep_sem.at[1]),
    ]
    for c in keeps:
        c.start()

    def part(kind, e, dst):
        def tile(i, _):
            cols = pl.ds(pl.multiple_of(i * TILE, TILE), TILE)
            if kind == 2:
                v = lax.dot_general(
                    rows_dy[e], wd[e, cols, :], (((1,), (1,)), ((), ())),
                    preferred_element_type=F32,
                )
            else:
                w = wg if kind == 0 else wu
                v = jnp.dot(rows_in[e], w[e, :, cols], preferred_element_type=F32)
            dst[:, cols] = v.astype(BF16)
            return 0

        lax.fori_loop(0, ffw // TILE, tile, 0)

    chunks = [(kind, j) for j in range(count // 2) for kind in (0, 1)]
    chunks += [(2, j) for j in range(count // 2)]
    core_copies, y_copies, loaded = [], [], set()

    def chunk_away(i):
        kind, j = chunks[i]
        if kind not in loaded:
            loads[kind].wait()
            loaded.add(kind)
        part(kind, 2 * j + 1 - core, away.at[i])
        core_copies.append(remote(away.at[i], near.at[i], core_send, core_recv, i, core_peer))
        core_copies[i].start()

    rows = rows_in.shape[1]
    step = 32

    def chunk_sum(i):
        core_copies[i].wait_recv()

        def some(r, _):
            at = pl.ds(pl.multiple_of(r * step, step), step)
            v = own[i, at, :].astype(F32) + near[i, at, :].astype(F32)
            own[i, at, :] = v.astype(BF16)
            return 0

        lax.fori_loop(0, rows // step, some, 0)
        y_copies.append(remote(own.at[i], far.at[i], y_send, y_recv, i, y_peer))
        y_copies[i].start()

    for i, (kind, j) in enumerate(chunks):
        chunk_away(i)
        if i > 0:
            chunk_sum(i - 1)
        part(kind, 2 * j + core, own.at[i])
    chunk_sum(len(chunks) - 1)

    pick_all[...] = jnp.zeros_like(pick_all)
    weighted_all[...] = jnp.zeros_like(weighted_all)
    for b in range(n_ex):
        pick, weighted = block_tables(routes[b], first_expert, count, top)
        for e in range(count):
            r = slice(e * CAP, (e + 1) * CAP)
            o = (e, slice(b * CAP, (b + 1) * CAP), slice(b * tok, (b + 1) * tok))
            pick_all[o] = pick[r].astype(BF16)
            weighted_all[o] = weighted[r].astype(BF16)
    keeps += [
        pltpu.make_async_copy(pick_all, pick_out, keep_sem.at[2]),
        pltpu.make_async_copy(weighted_all, weighted_out, keep_sem.at[3]),
    ]
    for c in keeps[2:]:
        c.start()

    shares = []

    def share(src, dst, i, j):
        e = 2 * j + core
        shares.append(remote(src.at[j], dst.at[e], share_send, share_recv, i, core_peer))
        shares[-1].start()
        keeps.append(pltpu.make_async_copy(src.at[j], dst.at[e], share_keep.at[i]))
        keeps[-1].start()

    def total(i, at):
        return own[i, at, :].astype(F32) + far[i, at, :].astype(F32)

    pairs = count // 2
    for j in range(pairs):
        y_copies[2 * j].wait_recv()
        y_copies[2 * j + 1].wait_recv()

        def forward(r, _):
            at = pl.ds(pl.multiple_of(r * step, step), step)
            g = total(2 * j, at)
            hidden[j, at, :] = (g * jax.nn.sigmoid(g) * total(2 * j + 1, at)).astype(BF16)
            return 0

        lax.fori_loop(0, rows // step, forward, 0)
        share(hidden, hidden_out, j, j)
    for j in range(pairs):
        y_copies[2 * pairs + j].wait_recv()

        def backward(r, _):
            at = pl.ds(pl.multiple_of(r * step, step), step)
            g, u, h = total(2 * j, at), total(2 * j + 1, at), total(2 * pairs + j, at)
            logistic = jax.nn.sigmoid(g)
            up_grad[j, at, :] = (h * g * logistic).astype(BF16)
            gate_grad[j, at, :] = (h * u * logistic * (1.0 + g * (1.0 - logistic))).astype(BF16)
            return 0

        lax.fori_loop(0, rows // step, backward, 0)
        share(gate_grad, gate_grad_out, pairs + 2 * j, j)
        share(up_grad, up_grad_out, pairs + 2 * j + 1, j)

    for c in copies.values():
        c.wait_send()
    for c in core_copies + y_copies:
        c.wait_send()
    for c in shares + keeps:
        c.wait()


def front(both, route, w_gate, w_up, w_down, n_ex):
    count, width, ffw = w_gate.shape
    rows = n_ex * CAP
    tok = both.shape[0]
    chunks = 3 * count // 2
    pairs = count // 2
    shape = jax.ShapeDtypeStruct
    vmem = pl.BlockSpec(memory_space=pltpu.VMEM)
    hbm = pl.BlockSpec(memory_space=pl.ANY)
    dma = pltpu.SemaphoreType.DMA
    return pl.pallas_call(
        front_kernel,
        out_shape=[
            shape((count, rows, width), BF16),
            shape((count, rows, width), BF16),
            shape((count, rows, n_ex * tok), BF16),
            shape((count, rows, n_ex * tok), BF16),
            shape((count, rows, ffw), BF16),
            shape((count, rows, ffw), BF16),
            shape((count, rows, ffw), BF16),
        ],
        in_specs=[vmem, vmem, hbm, hbm, hbm],
        out_specs=[hbm] * 7,
        scratch_shapes=[
            pltpu.VMEM(w_gate.shape, BF16),
            pltpu.VMEM(w_up.shape, BF16),
            pltpu.VMEM(w_down.shape, BF16),
            pltpu.VMEM((n_ex,) + both.shape, BF16),
            pltpu.VMEM((n_ex,) + route.shape, F32),
            pltpu.VMEM((count, rows, width), BF16),
            pltpu.VMEM((count, rows, width), BF16),
            pltpu.VMEM((count, rows, n_ex * tok), BF16),
            pltpu.VMEM((count, rows, n_ex * tok), BF16),
        ]
        + [pltpu.VMEM((chunks, rows, ffw), BF16)] * 4
        + [pltpu.VMEM((pairs, rows, ffw), BF16)] * 3
        + [dma((3,)), dma((4,))]
        + [dma((n_ex,))] * 4
        + [dma((chunks,))] * 4
        + [dma((3 * pairs,))] * 3,
        compiler_params=pltpu.CompilerParams(
            collective_id=0, has_side_effects=True, vmem_limit_bytes=58 * 1024 * 1024
        ),
        cost_estimate=pl.CostEstimate(
            flops=6 * count * rows * width * ffw, bytes_accessed=64 << 20, transcendentals=0
        ),
        name="front",
    )(both, route, w_gate, w_up, w_down)


def front_general(both, route, w_gate, w_up, w_down, n_ex):
    count, width, _ = w_gate.shape
    rows = n_ex * CAP
    top = route.shape[1] // 2
    route = lax.all_gather(route, "expert", axis=0, tiled=True)
    both = lax.all_gather(both, "expert", axis=0, tiled=True)
    pick, weighted, row_gate = tables(
        route[:, :top].astype(jnp.int32),
        route[:, top:],
        lax.axis_index("expert") * count,
        count,
        n_ex,
    )
    picked = mm(pick, both)
    rows_in = picked[:, :width].astype(BF16).reshape(count, rows, width)
    rows_dy = (picked[:, width:] * row_gate).astype(BF16).reshape(count, rows, width)

    def gate_up(e, w):
        return mm(rows_in[e], w[e]).astype(BF16)

    def back(e):
        return mm(rows_dy[e], w_down[e], ((1,), (1,))).astype(BF16)

    def forward(gate_sum, up_sum):
        logistic = jax.nn.sigmoid(gate_sum)
        return (gate_sum * logistic * up_sum).astype(BF16)

    def backward(gate_sum, up_sum, hidden_grad):
        logistic = jax.nn.sigmoid(gate_sum)
        up_grad = (hidden_grad * gate_sum * logistic).astype(BF16)
        gate_grad = (
            hidden_grad * up_sum * logistic * (1.0 + gate_sum * (1.0 - logistic))
        ).astype(BF16)
        return gate_grad, up_grad

    gate_sum, up_sum, hidden_grad = (
        lax.psum(jnp.stack(p), "dp").astype(F32)
        for p in (
            [gate_up(e, w_gate) for e in range(count)],
            [gate_up(e, w_up) for e in range(count)],
            [back(e) for e in range(count)],
        )
    )
    hidden = forward(gate_sum, up_sum)
    gate_grad, up_grad = backward(gate_sum, up_sum, hidden_grad)

    return rows_in, rows_dy, pick, weighted, hidden, gate_grad, up_grad


def make_body(n_dp, n_ex):
    fast = n_dp == 4 and n_ex == 8

    def body(tokens, expert_ids, gate_weights, w_gate, w_up, w_down, cotangent):
        width = tokens.shape[1]
        count = w_gate.shape[0]
        rows = n_ex * CAP
        both = jnp.concatenate([tokens, cotangent], axis=1)
        route = jnp.concatenate([expert_ids.astype(F32), gate_weights], axis=1)
        if fast:
            rows_in, rows_dy, pick, weighted, hidden, gate_grad, up_grad = front(
                both, route.T, w_gate, w_up, w_down, n_ex
            )
            pick = pick.reshape(count * rows, -1)
            weighted = weighted.reshape(count * rows, -1)
        else:
            rows_in, rows_dy, pick, weighted, hidden, gate_grad, up_grad = front_general(
                both, route, w_gate, w_up, w_down, n_ex
            )

        out_rows = jnp.concatenate([mm(hidden[e], w_down[e]).astype(BF16) for e in range(count)])
        mixed = mm(weighted, out_rows, ((0,), (0,))).astype(BF16)
        row_grad = jnp.concatenate(
            [
                (
                    mm(gate_grad[e], w_gate[e], ((1,), (1,))) + mm(up_grad[e], w_up[e], ((1,), (1,)))
                ).astype(BF16)
                for e in range(count)
            ]
        )
        token_grad = mm(pick, row_grad, ((0,), (0,))).astype(BF16)
        if fast:
            mixed, token_grad = return_sum(mixed, n_ex), return_sum(token_grad, n_ex)
        else:
            mixed, token_grad = (
                lax.psum_scatter(v, "expert", scatter_dimension=0, tiled=True)
                for v in (mixed, token_grad)
            )
        grad_gate = jnp.einsum(
            "erd,erf->edf", rows_in, gate_grad, preferred_element_type=F32
        ).astype(BF16)
        grad_up = jnp.einsum(
            "erd,erf->edf", rows_in, up_grad, preferred_element_type=F32
        ).astype(BF16)
        grad_down = jnp.einsum(
            "erf,erd->efd", hidden, rows_dy, preferred_element_type=F32
        ).astype(BF16)
        return mixed, token_grad, grad_gate, grad_up, grad_down

    return body


def solution(mesh):
    placed = (
        P("expert", "dp"),
        P("expert", None),
        P("expert", None),
        P("expert", "dp", None),
        P("expert", "dp", None),
        P("expert", None, "dp"),
        P("expert", "dp"),
    )
    return jax.shard_map(
        make_body(mesh.shape["dp"], mesh.shape["expert"]),
        mesh=mesh,
        in_specs=placed,
        out_specs=(
            P("expert", "dp"),
            P("expert", "dp"),
            P("expert", "dp", None),
            P("expert", "dp", None),
            P("expert", None, "dp"),
        ),
        check_vma=False,
    )
```

```python
import jax
import jax.numpy as jnp
from jax import lax
from jax.experimental import pallas as pl
from jax.experimental.pallas import tpu as pltpu
from jax.sharding import PartitionSpec as P

EXPERTS = 32
CAP = 32
F32 = jnp.float32
BF16 = jnp.bfloat16


def mm(a, b, dims=((1,), (0,))):
    return lax.dot_general(a, b, (dims, ((), ())), preferred_element_type=F32)


def tables(ids_all, gates_all, first_expert, local_count, blocks):
    tok = ids_all.shape[0] // blocks
    mine = first_expert + jnp.arange(local_count, dtype=jnp.int32)
    hits = ids_all[None, :, :] == mine[:, None, None]
    named = jnp.any(hits, axis=2).reshape(local_count, blocks, tok)
    gate = jnp.sum(jnp.where(hits, gates_all[None], 0.0), axis=2).reshape(local_count, blocks, tok)
    earlier = jnp.triu(jnp.ones((tok, tok), BF16), 1)
    rank = jnp.einsum("ebs,st->ebt", named.astype(BF16), earlier, preferred_element_type=F32)
    slot = jnp.arange(CAP, dtype=jnp.int32)
    block = jnp.arange(blocks, dtype=jnp.int32)
    where = jnp.where(named, rank.astype(jnp.int32), -1)
    pick = (where[:, None, None, :, :] == slot[None, None, :, None, None]) & (
        block[None, :, None, None, None] == block[None, None, None, :, None]
    )
    shape = (local_count * blocks * CAP, blocks * tok)
    weighted = jnp.where(pick, gate[:, None, None, :, :], 0.0)
    row_gate = jnp.sum(weighted, axis=(3, 4)).reshape(-1, 1)
    return pick.astype(BF16).reshape(shape), weighted.astype(BF16).reshape(shape), row_gate


def send(x, axis, pairs):
    return lax.ppermute(x, axis, pairs)


def flip(size, bit):
    return [(i, i ^ bit) for i in range(size)]


def add_column(parts, n_ex):
    n_z = n_ex // 2
    got = send(parts[n_z:], "expert", flip(n_ex, 1))
    return (parts[:n_z].astype(F32) + got.astype(F32)).astype(BF16)


def add_along(col, n_ex):
    total = col[0].astype(F32)
    for k in range(1, n_ex // 2):
        to = [(i, (i - 2 * k) % n_ex) for i in range(n_ex)]
        total += send(col[k], "expert", to).astype(F32)
    return total.astype(BF16)


TILE = 256


def block_tables(route, first_expert, local_count, top):
    tok = route.shape[1]
    rows = local_count * CAP
    number = lax.broadcasted_iota(jnp.int32, (rows, tok), 0)
    wanted = (first_expert + number // CAP).astype(F32)
    named = jnp.zeros((rows, tok), F32)
    gate = jnp.zeros((rows, tok), F32)
    for k in range(top):
        hit = route[k : k + 1, :] == wanted
        named = jnp.where(hit, 1.0, named)
        gate = jnp.where(hit, route[top + k : top + k + 1, :], gate)
    before = lax.broadcasted_iota(jnp.int32, (tok, tok), 0)
    after = lax.broadcasted_iota(jnp.int32, (tok, tok), 1)
    earlier = jnp.where(before < after, 1.0, 0.0).astype(BF16)
    rank = jnp.dot(named.astype(BF16), earlier, preferred_element_type=F32)
    pick = jnp.where(rank == (number % CAP).astype(F32), named, 0.0)
    return pick, pick * gate


def groups(n_z):
    place = [0] + list(range(2, n_z + 1)) + [1] + list(range(n_z + 1, 2 * n_z))
    cut = [0, 2 * CAP, (n_z + 1) * CAP, 2 * n_z * CAP]
    return place, cut


def front_kernel(
    both_ref, route_ref, wg_hbm, wu_hbm, wd_hbm,
    mixed_ref, token_out, rows_in_out, rows_dy_out, hidden_out, gate_grad_out, up_grad_out,
    wg, wu, wd, gathered, routes, rows_in, rows_dy, picks, weights,
    away, own, near, far, hidden, gate_grad, up_grad, results, partial, token_partial, from_x, from_z,
    load_sem, keep_sem, tok_send, tok_recv, route_send, route_recv,
    core_send, core_recv, y_send, y_recv, share_send, share_recv, ret_send, ret_recv,
):
    count, width, ffw = wg.shape
    n_ex = gathered.shape[0]
    n_z = n_ex // 2
    pairs = count // 2
    top = route_ref.shape[0] // 2
    position, cut = groups(n_z)
    dp = lax.axis_index("dp")
    me = lax.axis_index("expert")
    z = me // 2
    x = me % 2
    core = dp % 2
    x_peer = (dp, z * 2 + 1 - x)
    core_peer = (dp + 1 - 2 * core, me)
    y_peer = ((dp + 2) % 4, me)
    z_peers = [(dp, ((z + k) % n_z) * 2 + x) for k in range(1, n_z)]
    first_expert = me * count

    loads = [
        pltpu.make_async_copy(a, b, load_sem.at[i])
        for i, (a, b) in enumerate(((wg_hbm, wg), (wu_hbm, wu), (wd_hbm, wd)))
    ]
    for c in loads:
        c.start()

    barrier = pltpu.get_barrier_semaphore()
    peers = [x_peer, core_peer, y_peer] + z_peers
    for p in peers:
        pl.semaphore_signal(barrier, inc=1, device_id=p, device_id_type=pl.DeviceIdType.MESH)
    pl.semaphore_wait(barrier, len(peers))

    def remote(src, dst, s, r, i, to):
        return pltpu.make_async_remote_copy(
            src_ref=src, dst_ref=dst, send_sem=s.at[i], recv_sem=r.at[i],
            device_id=to, device_id_type=pl.DeviceIdType.MESH,
        )

    copies = {}
    kinds = (
        ("route", route_ref, routes, route_send, route_recv),
        ("tok", both_ref, gathered, tok_send, tok_recv),
    )
    for name, src, dst, s, r in kinds:
        copies[name, n_z] = remote(src, dst.at[n_z], s, r, n_z, x_peer)
        copies[name, n_z].start()
        for k in range(1, n_z):
            copies[name, k] = remote(src, dst.at[k], s, r, k, z_peers[k - 1])
            copies[name, k].start()

    def place(p, route, block):
        pick, weighted = block_tables(route, first_expert, count, top)
        picks[p] = pick.astype(BF16)
        weights[p] = weighted.astype(BF16)
        row_gate = jnp.sum(weighted, axis=1, keepdims=True)
        sel = pick.astype(BF16)
        at = slice(position[p] * CAP, (position[p] + 1) * CAP)
        a = jnp.dot(sel, block[:, :width], preferred_element_type=F32).astype(BF16)
        d = jnp.dot(sel, block[:, width:], preferred_element_type=F32) * row_gate
        d = d.astype(BF16)
        for e in range(count):
            rows_in[e, at, :] = a[e * CAP : (e + 1) * CAP]
            rows_dy[e, at, :] = d[e * CAP : (e + 1) * CAP]

    def arrived(p):
        copies["route", p].wait_recv()
        copies["tok", p].wait_recv()

    def column():
        for k in range(1, n_z):
            arrived(k)
            for name, _, buf, s, r in kinds:
                c = remote(buf.at[k], buf.at[n_z + k], s, r, n_z + k, x_peer)
                copies[name, n_z + k] = c
                c.start()
        for k in range(1, n_z):
            place(k, routes[k], gathered.at[k])

    def other_column():
        for k in range(1, n_z):
            arrived(n_z + k)
            place(n_z + k, routes[n_z + k], gathered.at[n_z + k])

    keeps = []

    def keep(src, dst):
        keeps.append(pltpu.make_async_copy(src, dst, keep_sem.at[len(keeps)]))
        keeps[-1].start()

    def part(kind, e, at, dst):
        def tile(i, _):
            cols = pl.ds(pl.multiple_of(i * TILE, TILE), TILE)
            if kind == 2:
                v = lax.dot_general(
                    rows_dy[e, at, :], wd[e, cols, :], (((1,), (1,)), ((), ())),
                    preferred_element_type=F32,
                )
            else:
                w = wg if kind == 0 else wu
                v = jnp.dot(rows_in[e, at, :], w[e, :, cols], preferred_element_type=F32)
            dst[at, cols] = v.astype(BF16)
            return 0

        lax.fori_loop(0, ffw // TILE, tile, 0)

    step = 32
    spans = [slice(cut[g], cut[g + 1]) for g in range(3)]
    core_copies, y_copies, loaded = {}, {}, set()

    def send_part(chunk):
        g, kind, j = chunk
        if kind not in loaded:
            loads[kind].wait()
            loaded.add(kind)
        i = kind * pairs + j
        part(kind, 2 * j + 1 - core, spans[g], away.at[i])
        c = remote(
            away.at[i, spans[g]], near.at[i, spans[g]], core_send, core_recv,
            g * 3 * pairs + i, core_peer,
        )
        core_copies[chunk] = c
        c.start()

    def each(g, f):
        def some(r, _):
            f(pl.ds(pl.multiple_of(cut[g] + r * step, step), step))
            return 0

        lax.fori_loop(0, (cut[g + 1] - cut[g]) // step, some, 0)

    def send_sum(chunk):
        g, kind, j = chunk
        i = kind * pairs + j
        core_copies[chunk].wait_recv()

        def add(at):
            v = own[i, at, :].astype(F32) + near[i, at, :].astype(F32)
            own[i, at, :] = v.astype(BF16)

        each(g, add)
        c = remote(
            own.at[i, spans[g]], far.at[i, spans[g]], y_send, y_recv,
            g * 3 * pairs + i, y_peer,
        )
        y_copies[chunk] = c
        c.start()

    def run(chunks):
        for i, chunk in enumerate(chunks):
            g, kind, j = chunk
            send_part(chunk)
            if i > 0:
                send_sum(chunks[i - 1])
            part(kind, 2 * j + core, spans[g], own.at[kind * pairs + j])
        send_sum(chunks[-1])

    shares = {}

    def share(buf, e, g, i):
        c = remote(
            buf.at[e, spans[g]], buf.at[e, spans[g]], share_send, share_recv,
            g * 3 * pairs + i, core_peer,
        )
        shares[g, i] = c
        c.start()

    def total(kind, j, at):
        i = kind * pairs + j
        return own[i, at, :].astype(F32) + far[i, at, :].astype(F32)

    def forward(g):
        for j in range(pairs):
            e = 2 * j + core
            y_copies[g, 0, j].wait_recv()
            y_copies[g, 1, j].wait_recv()

            def some(at):
                v = total(0, j, at)
                hidden[e, at, :] = (v * jax.nn.sigmoid(v) * total(1, j, at)).astype(BF16)

            each(g, some)
            share(hidden, e, g, j)

    def backward(g):
        for j in range(pairs):
            e = 2 * j + core
            y_copies[g, 2, j].wait_recv()

            def some(at):
                v, u, h = total(0, j, at), total(1, j, at), total(2, j, at)
                s = jax.nn.sigmoid(v)
                up_grad[e, at, :] = (h * v * s).astype(BF16)
                gate_grad[e, at, :] = (h * u * s * (1.0 + v * (1.0 - s))).astype(BF16)

            each(g, some)
            share(gate_grad, e, g, pairs + j)
            share(up_grad, e, g, 2 * pairs + j)

    col_tiles = [(c, min(c + TILE, width)) for c in range(0, width, TILE)]

    def row_grads(at):
        def one(e, _):
            for a, b in col_tiles:
                dims = (((1,), (1,)), ((), ()))
                v = lax.dot_general(
                    gate_grad[e, at, :], wg[e, a:b, :], dims, preferred_element_type=F32
                ) + lax.dot_general(
                    up_grad[e, at, :], wu[e, a:b, :], dims, preferred_element_type=F32
                )
                results[e, at, a:b] = v.astype(BF16)
            return 0

        lax.fori_loop(0, count, one, 0)

    def to_tokens(tables, out):
        for p in range(n_ex):
            at = slice(position[p] * CAP, (position[p] + 1) * CAP)
            rows = jnp.concatenate([results[e, at, :] for e in range(count)], axis=0)
            v = lax.dot_general(
                tables[p], rows, (((0,), (0,)), ((), ())), preferred_element_type=F32
            )
            out[p] = v.astype(BF16)

    place(0, route_ref[...], both_ref)
    arrived(n_z)
    place(n_z, routes[n_z], gathered.at[n_z])
    every = range(pairs)
    run([(0, kind, j) for j in every for kind in (0, 1)] + [(0, 2, j) for j in every])
    column()
    run([(1, kind, j) for j in every for kind in (0, 1)])
    other_column()
    keep(rows_in, rows_in_out)
    keep(rows_dy, rows_dy_out)
    run(
        [(2, kind, j) for j in every for kind in (0, 1)]
        + [(1, 2, j) for j in every]
        + [(2, 2, j) for j in every]
    )
    forward(0)
    backward(0)
    forward(1)
    forward(2)
    for g in range(3):
        for j in every:
            shares[g, j].wait_recv()
    keep(hidden, hidden_out)

    def out_rows(e, _):
        for a, b in col_tiles:
            v = jnp.dot(hidden[e], wd[e, :, a:b], preferred_element_type=F32)
            results[e, :, a:b] = v.astype(BF16)
        return 0

    lax.fori_loop(0, count, out_rows, 0)
    to_tokens(weights, partial)
    across = remote(partial.at[n_z:], from_x, ret_send, ret_recv, 0, x_peer)
    across.start()
    backward(1)
    for g in range(2):
        for i in range(pairs, 3 * pairs):
            shares[g, i].wait_recv()
    row_grads(slice(0, cut[2]))
    across.wait_recv()
    for k in range(n_z):
        v = partial[k].astype(F32) + from_x[k].astype(F32)
        partial[k] = v.astype(BF16)
    along = []
    for k in range(1, n_z):
        along.append(
            remote(
                partial.at[k], from_z.at[k - 1], ret_send, ret_recv, k, z_peers[n_z - k - 1]
            )
        )
        along[-1].start()
    backward(2)
    for i in range(pairs, 3 * pairs):
        shares[2, i].wait_recv()
    keep(gate_grad, gate_grad_out)
    keep(up_grad, up_grad_out)
    row_grads(spans[2])
    to_tokens(picks, token_partial)
    keep(token_partial, token_out)
    v = partial[0].astype(F32)
    for k, c in enumerate(along):
        c.wait_recv()
        v += from_z[k].astype(F32)
    mixed_ref[...] = v.astype(BF16)

    for group in (copies, core_copies, y_copies, shares):
        for c in group.values():
            c.wait_send()
    for c in [across] + along:
        c.wait_send()
    for c in keeps:
        c.wait()


def front(both, route, w_gate, w_up, w_down, n_ex):
    count, width, ffw = w_gate.shape
    rows = n_ex * CAP
    tok = both.shape[0]
    pairs = count // 2
    n_z = n_ex // 2
    shape = jax.ShapeDtypeStruct
    vmem = pl.BlockSpec(memory_space=pltpu.VMEM)
    hbm = pl.BlockSpec(memory_space=pl.ANY)
    dma = pltpu.SemaphoreType.DMA
    return pl.pallas_call(
        front_kernel,
        out_shape=[
            shape((tok, width), BF16),
            shape((n_ex, tok, width), BF16),
            shape((count, rows, width), BF16),
            shape((count, rows, width), BF16),
            shape((count, rows, ffw), BF16),
            shape((count, rows, ffw), BF16),
            shape((count, rows, ffw), BF16),
        ],
        in_specs=[vmem, vmem, hbm, hbm, hbm],
        out_specs=[vmem] + [hbm] * 6,
        scratch_shapes=[
            pltpu.VMEM(w_gate.shape, BF16),
            pltpu.VMEM(w_up.shape, BF16),
            pltpu.VMEM(w_down.shape, BF16),
            pltpu.VMEM((n_ex,) + both.shape, BF16),
            pltpu.VMEM((n_ex,) + route.shape, F32),
            pltpu.VMEM((count, rows, width), BF16),
            pltpu.VMEM((count, rows, width), BF16),
            pltpu.VMEM((n_ex, count * CAP, tok), BF16),
            pltpu.VMEM((n_ex, count * CAP, tok), BF16),
        ]
        + [pltpu.VMEM((3 * pairs, rows, ffw), BF16)] * 4
        + [pltpu.VMEM((count, rows, ffw), BF16)] * 3
        + [pltpu.VMEM((count, rows, width), BF16)]
        + [pltpu.VMEM((n_ex, tok, width), BF16)] * 2
        + [pltpu.VMEM((n_z, tok, width), BF16), pltpu.VMEM((n_z - 1, tok, width), BF16)]
        + [dma((3,)), dma((6,))]
        + [dma((n_ex,))] * 4
        + [dma((9 * pairs,))] * 6
        + [dma((n_z,))] * 2,
        compiler_params=pltpu.CompilerParams(
            collective_id=0, has_side_effects=True, vmem_limit_bytes=60 * 1024 * 1024
        ),
        cost_estimate=pl.CostEstimate(
            flops=12 * count * rows * width * ffw, bytes_accessed=64 << 20, transcendentals=0
        ),
        name="front",
    )(both, route, w_gate, w_up, w_down)


def front_general(both, route, w_gate, w_up, w_down, n_ex):
    count, width, _ = w_gate.shape
    rows = n_ex * CAP
    top = route.shape[1] // 2
    route = lax.all_gather(route, "expert", axis=0, tiled=True)
    both = lax.all_gather(both, "expert", axis=0, tiled=True)
    pick, weighted, row_gate = tables(
        route[:, :top].astype(jnp.int32),
        route[:, top:],
        lax.axis_index("expert") * count,
        count,
        n_ex,
    )
    picked = mm(pick, both)
    rows_in = picked[:, :width].astype(BF16).reshape(count, rows, width)
    rows_dy = (picked[:, width:] * row_gate).astype(BF16).reshape(count, rows, width)

    def gate_up(e, w):
        return mm(rows_in[e], w[e]).astype(BF16)

    def back(e):
        return mm(rows_dy[e], w_down[e], ((1,), (1,))).astype(BF16)

    def forward(gate_sum, up_sum):
        logistic = jax.nn.sigmoid(gate_sum)
        return (gate_sum * logistic * up_sum).astype(BF16)

    def backward(gate_sum, up_sum, hidden_grad):
        logistic = jax.nn.sigmoid(gate_sum)
        up_grad = (hidden_grad * gate_sum * logistic).astype(BF16)
        gate_grad = (
            hidden_grad * up_sum * logistic * (1.0 + gate_sum * (1.0 - logistic))
        ).astype(BF16)
        return gate_grad, up_grad

    gate_sum, up_sum, hidden_grad = (
        lax.psum(jnp.stack(p), "dp").astype(F32)
        for p in (
            [gate_up(e, w_gate) for e in range(count)],
            [gate_up(e, w_up) for e in range(count)],
            [back(e) for e in range(count)],
        )
    )
    hidden = forward(gate_sum, up_sum)
    gate_grad, up_grad = backward(gate_sum, up_sum, hidden_grad)

    return rows_in, rows_dy, pick, weighted, hidden, gate_grad, up_grad


def weight_grad(a, b):
    return jnp.einsum("erm,ern->emn", a, b, preferred_element_type=F32).astype(BF16)


def make_body(n_dp, n_ex):
    fast = n_dp == 4 and n_ex == 8

    def body(tokens, expert_ids, gate_weights, w_gate, w_up, w_down, cotangent):
        count = w_gate.shape[0]
        both = jnp.concatenate([tokens, cotangent], axis=1)
        route = jnp.concatenate([expert_ids.astype(F32), gate_weights], axis=1)
        if fast:
            mixed, parts, rows_in, rows_dy, hidden, gate_grad, up_grad = front(
                both, route.T, w_gate, w_up, w_down, n_ex
            )
            grad_down = weight_grad(hidden, rows_dy)
            col = add_column(parts, n_ex)
            rows_in, col = lax.optimization_barrier((rows_in, col))
            token_grad = add_along(col, n_ex)
        else:
            rows_in, rows_dy, pick, weighted, hidden, gate_grad, up_grad = front_general(
                both, route, w_gate, w_up, w_down, n_ex
            )
            out_rows = [mm(hidden[e], w_down[e]).astype(BF16) for e in range(count)]
            row_grad = [
                (
                    mm(gate_grad[e], w_gate[e], ((1,), (1,))) + mm(up_grad[e], w_up[e], ((1,), (1,)))
                ).astype(BF16)
                for e in range(count)
            ]
            mixed = mm(weighted, jnp.concatenate(out_rows), ((0,), (0,))).astype(BF16)
            token_grad = mm(pick, jnp.concatenate(row_grad), ((0,), (0,))).astype(BF16)
            mixed, token_grad = (
                lax.psum_scatter(v, "expert", scatter_dimension=0, tiled=True)
                for v in (mixed, token_grad)
            )
            grad_down = weight_grad(hidden, rows_dy)
        grad_gate = weight_grad(rows_in, gate_grad)
        grad_up = weight_grad(rows_in, up_grad)
        return mixed, token_grad, grad_gate, grad_up, grad_down

    return body


def solution(mesh):
    placed = (
        P("expert", "dp"),
        P("expert", None),
        P("expert", None),
        P("expert", "dp", None),
        P("expert", "dp", None),
        P("expert", None, "dp"),
        P("expert", "dp"),
    )
    return jax.shard_map(
        make_body(mesh.shape["dp"], mesh.shape["expert"]),
        mesh=mesh,
        in_specs=placed,
        out_specs=(
            P("expert", "dp"),
            P("expert", "dp"),
            P("expert", "dp", None),
            P("expert", "dp", None),
            P("expert", None, "dp"),
        ),
        check_vma=False,
    )
```

```python
import jax
import jax.numpy as jnp
from jax import lax
from jax.experimental import pallas as pl
from jax.experimental.pallas import tpu as pltpu
from jax.sharding import PartitionSpec as P

EXPERTS = 32
CAP = 32
F32 = jnp.float32
BF16 = jnp.bfloat16


def mm(a, b, dims=((1,), (0,))):
    return lax.dot_general(a, b, (dims, ((), ())), preferred_element_type=F32)


def tables(ids_all, gates_all, first_expert, local_count, blocks):
    tok = ids_all.shape[0] // blocks
    mine = first_expert + jnp.arange(local_count, dtype=jnp.int32)
    hits = ids_all[None, :, :] == mine[:, None, None]
    named = jnp.any(hits, axis=2).reshape(local_count, blocks, tok)
    gate = jnp.sum(jnp.where(hits, gates_all[None], 0.0), axis=2).reshape(local_count, blocks, tok)
    earlier = jnp.triu(jnp.ones((tok, tok), BF16), 1)
    rank = jnp.einsum("ebs,st->ebt", named.astype(BF16), earlier, preferred_element_type=F32)
    slot = jnp.arange(CAP, dtype=jnp.int32)
    block = jnp.arange(blocks, dtype=jnp.int32)
    where = jnp.where(named, rank.astype(jnp.int32), -1)
    pick = (where[:, None, None, :, :] == slot[None, None, :, None, None]) & (
        block[None, :, None, None, None] == block[None, None, None, :, None]
    )
    shape = (local_count * blocks * CAP, blocks * tok)
    weighted = jnp.where(pick, gate[:, None, None, :, :], 0.0)
    row_gate = jnp.sum(weighted, axis=(3, 4)).reshape(-1, 1)
    return pick.astype(BF16).reshape(shape), weighted.astype(BF16).reshape(shape), row_gate


def send(x, axis, pairs):
    return lax.ppermute(x, axis, pairs)


def add_along(col, n_ex):
    total = col[0].astype(F32)
    for k in range(1, n_ex // 2):
        to = [(i, (i - 2 * k) % n_ex) for i in range(n_ex)]
        total += send(col[k], "expert", to).astype(F32)
    return total.astype(BF16)


TILE = 256


def block_tables(route, first_expert, local_count, top):
    tok = route.shape[1]
    rows = local_count * CAP
    number = lax.broadcasted_iota(jnp.int32, (rows, tok), 0)
    wanted = (first_expert + number // CAP).astype(F32)
    named = jnp.zeros((rows, tok), F32)
    gate = jnp.zeros((rows, tok), F32)
    for k in range(top):
        hit = route[k : k + 1, :] == wanted
        named = jnp.where(hit, 1.0, named)
        gate = jnp.where(hit, route[top + k : top + k + 1, :], gate)
    before = lax.broadcasted_iota(jnp.int32, (tok, tok), 0)
    after = lax.broadcasted_iota(jnp.int32, (tok, tok), 1)
    earlier = jnp.where(before < after, 1.0, 0.0).astype(BF16)
    rank = jnp.dot(named.astype(BF16), earlier, preferred_element_type=F32)
    pick = jnp.where(rank == (number % CAP).astype(F32), named, 0.0)
    return pick, pick * gate


def groups(n_z):
    place = [0] + list(range(n_z + 1, 2 * n_z)) + [1] + list(range(2, n_z + 1))
    a, b, c = 2 * CAP, (n_z + 1) * CAP, 2 * n_z * CAP
    return place, (slice(0, a), slice(b, c), slice(a, b))


def front_kernel(
    tokens_ref, cot_ref, ids_ref, gates_ref, wg_hbm, wu_hbm, wd_hbm,
    mixed_ref, token_out, rows_in_out, rows_dy_out, hidden_out, gate_grad_out, up_grad_out,
    wg, wu, wd, gathered, routes, rows_in, rows_dy, picks, weights,
    away, own, near, far, hidden, gate_grad, up_grad, results, partial, token_partial, from_x, from_z, token_x,
    load_sem, keep_sem, tok_send, tok_recv, route_send, route_recv,
    core_send, core_recv, y_send, y_recv, share_send, share_recv, ret_send, ret_recv,
):
    count, width, ffw = wg.shape
    n_ex = gathered.shape[0]
    n_z = n_ex // 2
    pairs = count // 2
    top = ids_ref.shape[0]
    position, spans = groups(n_z)
    dp = lax.axis_index("dp")
    me = lax.axis_index("expert")
    z = me // 2
    x = me % 2
    core = dp % 2
    x_peer = (dp, z * 2 + 1 - x)
    core_peer = (dp + 1 - 2 * core, me)
    y_peer = ((dp + 2) % 4, me)
    z_peers = [(dp, ((z + k) % n_z) * 2 + x) for k in range(1, n_z)]
    first_expert = me * count

    loads = [
        pltpu.make_async_copy(a, b, load_sem.at[i])
        for i, (a, b) in enumerate(((wg_hbm, wg), (wu_hbm, wu), (wd_hbm, wd)))
    ]
    for c in loads:
        c.start()

    gathered[0, :, :width] = tokens_ref[...]
    gathered[0, :, width:] = cot_ref[...]
    routes[0, :top, :] = ids_ref[...].astype(F32)
    routes[0, top:, :] = gates_ref[...]

    barrier = pltpu.get_barrier_semaphore()
    peers = [x_peer, core_peer, y_peer] + z_peers
    for p in peers:
        pl.semaphore_signal(barrier, inc=1, device_id=p, device_id_type=pl.DeviceIdType.MESH)
    pl.semaphore_wait(barrier, len(peers))

    def remote(src, dst, s, r, i, to):
        return pltpu.make_async_remote_copy(
            src_ref=src, dst_ref=dst, send_sem=s.at[i], recv_sem=r.at[i],
            device_id=to, device_id_type=pl.DeviceIdType.MESH,
        )

    copies = {}
    kinds = (
        ("route", routes, route_send, route_recv),
        ("tok", gathered, tok_send, tok_recv),
    )
    for name, buf, s, r in kinds:
        copies[name, n_z] = remote(buf.at[0], buf.at[n_z], s, r, n_z, x_peer)
        copies[name, n_z].start()
        for k in range(1, n_z):
            copies[name, k] = remote(buf.at[0], buf.at[k], s, r, k, z_peers[k - 1])
            copies[name, k].start()

    def place(p):
        block = gathered.at[p]
        pick, weighted = block_tables(routes[p], first_expert, count, top)
        picks[p] = pick.astype(BF16)
        weights[p] = weighted.astype(BF16)
        row_gate = jnp.sum(weighted, axis=1, keepdims=True)
        sel = pick.astype(BF16)
        at = slice(position[p] * CAP, (position[p] + 1) * CAP)
        a = jnp.dot(sel, block[:, :width], preferred_element_type=F32).astype(BF16)
        d = jnp.dot(sel, block[:, width:], preferred_element_type=F32) * row_gate
        d = d.astype(BF16)
        for e in range(count):
            rows_in[e, at, :] = a[e * CAP : (e + 1) * CAP]
            rows_dy[e, at, :] = d[e * CAP : (e + 1) * CAP]

    def arrived(p):
        copies["route", p].wait_recv()
        copies["tok", p].wait_recv()

    def column():
        for k in range(1, n_z):
            arrived(k)
            for name, buf, s, r in kinds:
                c = remote(buf.at[k], buf.at[n_z + k], s, r, n_z + k, x_peer)
                copies[name, n_z + k] = c
                c.start()
            place(k)

    def other_column():
        for k in range(1, n_z):
            arrived(n_z + k)
            place(n_z + k)

    keeps = []

    def keep(src, dst):
        keeps.append(pltpu.make_async_copy(src, dst, keep_sem.at[len(keeps)]))
        keeps[-1].start()

    def part(kind, e, at, dst):
        def tile(i, _):
            cols = pl.ds(pl.multiple_of(i * TILE, TILE), TILE)
            if kind == 2:
                v = lax.dot_general(
                    rows_dy[e, at, :], wd[e, cols, :], (((1,), (1,)), ((), ())),
                    preferred_element_type=F32,
                )
            else:
                w = wg if kind == 0 else wu
                v = jnp.dot(rows_in[e, at, :], w[e, :, cols], preferred_element_type=F32)
            dst[at, cols] = v.astype(BF16)
            return 0

        lax.fori_loop(0, ffw // TILE, tile, 0)

    step = 32
    core_copies, y_copies, loaded = {}, {}, set()

    def send_part(chunk):
        g, kind, j = chunk
        if kind not in loaded:
            loads[kind].wait()
            loaded.add(kind)
        i = kind * pairs + j
        part(kind, 2 * j + 1 - core, spans[g], away.at[i])
        c = remote(
            away.at[i, spans[g]], near.at[i, spans[g]], core_send, core_recv,
            g * 3 * pairs + i, core_peer,
        )
        core_copies[chunk] = c
        c.start()

    def each(g, f):
        def some(r, _):
            f(pl.ds(pl.multiple_of(spans[g].start + r * step, step), step))
            return 0

        lax.fori_loop(0, (spans[g].stop - spans[g].start) // step, some, 0)

    def send_sum(chunk):
        g, kind, j = chunk
        i = kind * pairs + j
        core_copies[chunk].wait_recv()

        def add(at):
            v = own[i, at, :].astype(F32) + near[i, at, :].astype(F32)
            own[i, at, :] = v.astype(BF16)

        each(g, add)
        c = remote(
            own.at[i, spans[g]], far.at[i, spans[g]], y_send, y_recv,
            g * 3 * pairs + i, y_peer,
        )
        y_copies[chunk] = c
        c.start()

    def run(chunks):
        for i, chunk in enumerate(chunks):
            g, kind, j = chunk
            send_part(chunk)
            if i > 0:
                send_sum(chunks[i - 1])
            part(kind, 2 * j + core, spans[g], own.at[kind * pairs + j])
        send_sum(chunks[-1])

    shares = {}

    def share(buf, e, g, i):
        c = remote(
            buf.at[e, spans[g]], buf.at[e, spans[g]], share_send, share_recv,
            g * 3 * pairs + i, core_peer,
        )
        shares[g, i] = c
        c.start()

    def total(kind, j, at):
        i = kind * pairs + j
        return own[i, at, :].astype(F32) + far[i, at, :].astype(F32)

    def forward(g):
        for j in range(pairs):
            e = 2 * j + core
            y_copies[g, 0, j].wait_recv()
            y_copies[g, 1, j].wait_recv()

            def some(at):
                v = total(0, j, at)
                hidden[e, at, :] = (v * jax.nn.sigmoid(v) * total(1, j, at)).astype(BF16)

            each(g, some)
            share(hidden, e, g, j)

    def backward(g):
        for j in range(pairs):
            e = 2 * j + core
            y_copies[g, 2, j].wait_recv()

            def some(at):
                v, u, h = total(0, j, at), total(1, j, at), total(2, j, at)
                s = jax.nn.sigmoid(v)
                up_grad[e, at, :] = (h * v * s).astype(BF16)
                gate_grad[e, at, :] = (h * u * s * (1.0 + v * (1.0 - s))).astype(BF16)

            each(g, some)
            share(gate_grad, e, g, pairs + j)
            share(up_grad, e, g, 2 * pairs + j)

    col_tiles = [(c, min(c + TILE, width)) for c in range(0, width, TILE)]

    def row_grads(at):
        def one(e, _):
            for a, b in col_tiles:
                dims = (((1,), (1,)), ((), ()))
                v = lax.dot_general(
                    gate_grad[e, at, :], wg[e, a:b, :], dims, preferred_element_type=F32
                ) + lax.dot_general(
                    up_grad[e, at, :], wu[e, a:b, :], dims, preferred_element_type=F32
                )
                results[e, at, a:b] = v.astype(BF16)
            return 0

        lax.fori_loop(0, count, one, 0)

    def to_tokens(tables, out, slots):
        for p in slots:
            at = slice(position[p] * CAP, (position[p] + 1) * CAP)
            rows = jnp.concatenate([results[e, at, :] for e in range(count)], axis=0)
            v = lax.dot_general(
                tables[p], rows, (((0,), (0,)), ((), ())), preferred_element_type=F32
            )
            out[p] = v.astype(BF16)

    place(0)
    arrived(n_z)
    place(n_z)
    every = range(pairs)
    run([(0, kind, j) for j in every for kind in (0, 1)] + [(0, 2, j) for j in every])
    column()
    run([(1, kind, j) for j in every for kind in (0, 1)])
    other_column()
    keep(rows_in, rows_in_out)
    keep(rows_dy, rows_dy_out)
    run(
        [(2, kind, j) for j in every for kind in (0, 1)]
        + [(2, 2, j) for j in every]
        + [(1, 2, j) for j in every]
    )
    forward(0)
    backward(0)
    forward(1)
    forward(2)
    for g in range(3):
        for j in every:
            shares[g, j].wait_recv()
    keep(hidden, hidden_out)

    def out_rows(e, _):
        for a, b in col_tiles:
            v = jnp.dot(hidden[e], wd[e, :, a:b], preferred_element_type=F32)
            results[e, :, a:b] = v.astype(BF16)
        return 0

    lax.fori_loop(0, count, out_rows, 0)
    to_tokens(weights, partial, range(n_ex))
    across = remote(partial.at[n_z:], from_x, ret_send, ret_recv, 0, x_peer)
    across.start()
    backward(2)
    for g in (0, 2):
        for i in range(pairs, 3 * pairs):
            shares[g, i].wait_recv()
    row_grads(slice(0, spans[2].stop))
    to_tokens(picks, token_partial, range(n_z, n_ex))
    token_across = remote(token_partial.at[n_z:], token_x, ret_send, ret_recv, n_z, x_peer)
    token_across.start()

    def add_x(mine, other):
        for k in range(n_z):
            mine[k] = (mine[k].astype(F32) + other[k].astype(F32)).astype(BF16)

    across.wait_recv()
    add_x(partial, from_x)
    along = []
    for k in range(1, n_z):
        along.append(
            remote(
                partial.at[k], from_z.at[k - 1], ret_send, ret_recv, k, z_peers[n_z - k - 1]
            )
        )
        along[-1].start()
    backward(1)
    for i in range(pairs, 3 * pairs):
        shares[1, i].wait_recv()
    keep(gate_grad, gate_grad_out)
    keep(up_grad, up_grad_out)
    row_grads(spans[1])
    to_tokens(picks, token_partial, range(n_z))
    token_across.wait_recv()
    add_x(token_partial, token_x)
    keep(token_partial.at[:n_z], token_out)
    v = partial[0].astype(F32)
    for k, c in enumerate(along):
        c.wait_recv()
        v += from_z[k].astype(F32)
    mixed_ref[...] = v.astype(BF16)

    for group in (copies, core_copies, y_copies, shares):
        for c in group.values():
            c.wait_send()
    for c in [across, token_across] + along:
        c.wait_send()
    for c in keeps:
        c.wait()


def front(tokens, cotangent, ids, gates, w_gate, w_up, w_down, n_ex):
    count, width, ffw = w_gate.shape
    rows = n_ex * CAP
    tok = tokens.shape[0]
    pairs = count // 2
    n_z = n_ex // 2
    shape = jax.ShapeDtypeStruct
    vmem = pl.BlockSpec(memory_space=pltpu.VMEM)
    hbm = pl.BlockSpec(memory_space=pl.ANY)
    dma = pltpu.SemaphoreType.DMA
    return pl.pallas_call(
        front_kernel,
        out_shape=[
            shape((tok, width), BF16),
            shape((n_z, tok, width), BF16),
            shape((count, rows, width), BF16),
            shape((count, rows, width), BF16),
            shape((count, rows, ffw), BF16),
            shape((count, rows, ffw), BF16),
            shape((count, rows, ffw), BF16),
        ],
        in_specs=[vmem] * 4 + [hbm] * 3,
        out_specs=[vmem] + [hbm] * 6,
        scratch_shapes=[
            pltpu.VMEM(w_gate.shape, BF16),
            pltpu.VMEM(w_up.shape, BF16),
            pltpu.VMEM(w_down.shape, BF16),
            pltpu.VMEM((n_ex, tok, 2 * width), BF16),
            pltpu.VMEM((n_ex, 2 * ids.shape[0], tok), F32),
            pltpu.VMEM((count, rows, width), BF16),
            pltpu.VMEM((count, rows, width), BF16),
            pltpu.VMEM((n_ex, count * CAP, tok), BF16),
            pltpu.VMEM((n_ex, count * CAP, tok), BF16),
        ]
        + [pltpu.VMEM((3 * pairs, rows, ffw), BF16)] * 4
        + [pltpu.VMEM((count, rows, ffw), BF16)] * 3
        + [pltpu.VMEM((count, rows, width), BF16)]
        + [pltpu.VMEM((n_ex, tok, width), BF16)] * 2
        + [pltpu.VMEM((n_z, tok, width), BF16), pltpu.VMEM((n_z - 1, tok, width), BF16)]
        + [pltpu.VMEM((n_z, tok, width), BF16)]
        + [dma((3,)), dma((6,))]
        + [dma((n_ex,))] * 4
        + [dma((9 * pairs,))] * 6
        + [dma((n_z + 1,))] * 2,
        compiler_params=pltpu.CompilerParams(
            collective_id=0, has_side_effects=True, vmem_limit_bytes=60 * 1024 * 1024
        ),
        cost_estimate=pl.CostEstimate(
            flops=12 * count * rows * width * ffw, bytes_accessed=64 << 20, transcendentals=0
        ),
        name="front",
    )(tokens, cotangent, ids, gates, w_gate, w_up, w_down)


def front_general(both, route, w_gate, w_up, w_down, n_ex):
    count, width, _ = w_gate.shape
    rows = n_ex * CAP
    top = route.shape[1] // 2
    route = lax.all_gather(route, "expert", axis=0, tiled=True)
    both = lax.all_gather(both, "expert", axis=0, tiled=True)
    pick, weighted, row_gate = tables(
        route[:, :top].astype(jnp.int32),
        route[:, top:],
        lax.axis_index("expert") * count,
        count,
        n_ex,
    )
    picked = mm(pick, both)
    rows_in = picked[:, :width].astype(BF16).reshape(count, rows, width)
    rows_dy = (picked[:, width:] * row_gate).astype(BF16).reshape(count, rows, width)

    def gate_up(e, w):
        return mm(rows_in[e], w[e]).astype(BF16)

    def back(e):
        return mm(rows_dy[e], w_down[e], ((1,), (1,))).astype(BF16)

    def forward(gate_sum, up_sum):
        logistic = jax.nn.sigmoid(gate_sum)
        return (gate_sum * logistic * up_sum).astype(BF16)

    def backward(gate_sum, up_sum, hidden_grad):
        logistic = jax.nn.sigmoid(gate_sum)
        up_grad = (hidden_grad * gate_sum * logistic).astype(BF16)
        gate_grad = (
            hidden_grad * up_sum * logistic * (1.0 + gate_sum * (1.0 - logistic))
        ).astype(BF16)
        return gate_grad, up_grad

    gate_sum, up_sum, hidden_grad = (
        lax.psum(jnp.stack(p), "dp").astype(F32)
        for p in (
            [gate_up(e, w_gate) for e in range(count)],
            [gate_up(e, w_up) for e in range(count)],
            [back(e) for e in range(count)],
        )
    )
    hidden = forward(gate_sum, up_sum)
    gate_grad, up_grad = backward(gate_sum, up_sum, hidden_grad)

    return rows_in, rows_dy, pick, weighted, hidden, gate_grad, up_grad


def weight_grad(a, b):
    return jnp.einsum("erm,ern->emn", a, b, preferred_element_type=F32).astype(BF16)


def make_body(n_dp, n_ex):
    fast = n_dp == 4 and n_ex == 8

    def body(tokens, expert_ids, gate_weights, w_gate, w_up, w_down, cotangent):
        count = w_gate.shape[0]
        if fast:
            mixed, col, rows_in, rows_dy, hidden, gate_grad, up_grad = front(
                tokens, cotangent, expert_ids.T, gate_weights.T, w_gate, w_up, w_down, n_ex
            )
            token_grad = add_along(col, n_ex)
        else:
            both = jnp.concatenate([tokens, cotangent], axis=1)
            route = jnp.concatenate([expert_ids.astype(F32), gate_weights], axis=1)
            rows_in, rows_dy, pick, weighted, hidden, gate_grad, up_grad = front_general(
                both, route, w_gate, w_up, w_down, n_ex
            )
            out_rows = [mm(hidden[e], w_down[e]).astype(BF16) for e in range(count)]
            row_grad = [
                (
                    mm(gate_grad[e], w_gate[e], ((1,), (1,))) + mm(up_grad[e], w_up[e], ((1,), (1,)))
                ).astype(BF16)
                for e in range(count)
            ]
            mixed = mm(weighted, jnp.concatenate(out_rows), ((0,), (0,))).astype(BF16)
            token_grad = mm(pick, jnp.concatenate(row_grad), ((0,), (0,))).astype(BF16)
            mixed, token_grad = (
                lax.psum_scatter(v, "expert", scatter_dimension=0, tiled=True)
                for v in (mixed, token_grad)
            )
        grad_down = weight_grad(hidden, rows_dy)
        grad_gate = weight_grad(rows_in, gate_grad)
        grad_up = weight_grad(rows_in, up_grad)
        return mixed, token_grad, grad_gate, grad_up, grad_down

    return body


def solution(mesh):
    placed = (
        P("expert", "dp"),
        P("expert", None),
        P("expert", None),
        P("expert", "dp", None),
        P("expert", "dp", None),
        P("expert", None, "dp"),
        P("expert", "dp"),
    )
    return jax.shard_map(
        make_body(mesh.shape["dp"], mesh.shape["expert"]),
        mesh=mesh,
        in_specs=placed,
        out_specs=(
            P("expert", "dp"),
            P("expert", "dp"),
            P("expert", "dp", None),
            P("expert", "dp", None),
            P("expert", None, "dp"),
        ),
        check_vma=False,
    )
```

```python
import jax
import jax.numpy as jnp
from jax import lax
from jax.experimental import pallas as pl
from jax.experimental.pallas import tpu as pltpu
from jax.sharding import PartitionSpec as P

EXPERTS = 32
CAP = 32
F32 = jnp.float32
BF16 = jnp.bfloat16


def mm(a, b, dims=((1,), (0,))):
    return lax.dot_general(a, b, (dims, ((), ())), preferred_element_type=F32)


def tables(ids_all, gates_all, first_expert, local_count, blocks):
    tok = ids_all.shape[0] // blocks
    mine = first_expert + jnp.arange(local_count, dtype=jnp.int32)
    hits = ids_all[None, :, :] == mine[:, None, None]
    named = jnp.any(hits, axis=2).reshape(local_count, blocks, tok)
    gate = jnp.sum(jnp.where(hits, gates_all[None], 0.0), axis=2).reshape(local_count, blocks, tok)
    earlier = jnp.triu(jnp.ones((tok, tok), BF16), 1)
    rank = jnp.einsum("ebs,st->ebt", named.astype(BF16), earlier, preferred_element_type=F32)
    slot = jnp.arange(CAP, dtype=jnp.int32)
    block = jnp.arange(blocks, dtype=jnp.int32)
    where = jnp.where(named, rank.astype(jnp.int32), -1)
    pick = (where[:, None, None, :, :] == slot[None, None, :, None, None]) & (
        block[None, :, None, None, None] == block[None, None, None, :, None]
    )
    shape = (local_count * blocks * CAP, blocks * tok)
    weighted = jnp.where(pick, gate[:, None, None, :, :], 0.0)
    row_gate = jnp.sum(weighted, axis=(3, 4)).reshape(-1, 1)
    return pick.astype(BF16).reshape(shape), weighted.astype(BF16).reshape(shape), row_gate


def send(x, axis, pairs):
    return lax.ppermute(x, axis, pairs)


def add_along(col, n_ex):
    total = col[0].astype(F32)
    for k in range(1, n_ex // 2):
        to = [(i, (i - 2 * k) % n_ex) for i in range(n_ex)]
        total += send(col[k], "expert", to).astype(F32)
    return total.astype(BF16)


TILE = 256


def block_tables(route, first_expert, local_count, top):
    tok = route.shape[1]
    rows = local_count * CAP
    number = lax.broadcasted_iota(jnp.int32, (rows, tok), 0)
    wanted = (first_expert + number // CAP).astype(F32)
    named = jnp.zeros((rows, tok), F32)
    gate = jnp.zeros((rows, tok), F32)
    for k in range(top):
        hit = route[k : k + 1, :] == wanted
        named = jnp.where(hit, 1.0, named)
        gate = jnp.where(hit, route[top + k : top + k + 1, :], gate)
    before = lax.broadcasted_iota(jnp.int32, (tok, tok), 0)
    after = lax.broadcasted_iota(jnp.int32, (tok, tok), 1)
    earlier = jnp.where(before < after, 1.0, 0.0).astype(BF16)
    rank = jnp.dot(named.astype(BF16), earlier, preferred_element_type=F32)
    pick = jnp.where(rank == (number % CAP).astype(F32), named, 0.0)
    return pick, pick * gate


def groups(n_z):
    place = [0] + list(range(n_z + 1, 2 * n_z)) + [1] + list(range(2, n_z + 1))
    a, b, c = 2 * CAP, (n_z + 1) * CAP, 2 * n_z * CAP
    return place, (slice(0, a), slice(b, c), slice(a, b))


def front_kernel(
    tokens_ref, cot_ref, ids_ref, gates_ref, wg_hbm, wu_hbm, wd_hbm,
    mixed_ref, token_out, rows_in_out, rows_dy_out, hidden_out, gate_grad_out, up_grad_out,
    wg, wu, wd, gathered, routes, rows_in, rows_dy, picks, weights,
    away, own, near, far, hidden, gate_grad, up_grad, results, partial, token_partial, from_x, from_z, token_x,
    load_sem, keep_sem, tok_send, tok_recv, route_send, route_recv,
    core_send, core_recv, y_send, y_recv, share_send, share_recv, ret_send, ret_recv,
):
    count, width, ffw = wg.shape
    n_ex = gathered.shape[0]
    n_z = n_ex // 2
    pairs = count // 2
    top = ids_ref.shape[0]
    position, spans = groups(n_z)
    dp = lax.axis_index("dp")
    me = lax.axis_index("expert")
    z = me // 2
    x = me % 2
    core = dp % 2
    x_peer = (dp, z * 2 + 1 - x)
    core_peer = (dp + 1 - 2 * core, me)
    y_peer = ((dp + 2) % 4, me)
    z_peers = [(dp, ((z + k) % n_z) * 2 + x) for k in range(1, n_z)]
    first_expert = me * count

    loads = [
        pltpu.make_async_copy(a, b, load_sem.at[i])
        for i, (a, b) in enumerate(((wg_hbm, wg), (wu_hbm, wu), (wd_hbm, wd)))
    ]
    for c in loads:
        c.start()

    gathered[0, :, :width] = tokens_ref[...]
    gathered[0, :, width:] = cot_ref[...]
    routes[0, :top, :] = ids_ref[...].astype(F32)
    routes[0, top:, :] = gates_ref[...]

    barrier = pltpu.get_barrier_semaphore()
    peers = [x_peer, core_peer, y_peer] + z_peers
    for p in peers:
        pl.semaphore_signal(barrier, inc=1, device_id=p, device_id_type=pl.DeviceIdType.MESH)
    pl.semaphore_wait(barrier, len(peers))

    def remote(src, dst, s, r, i, to):
        return pltpu.make_async_remote_copy(
            src_ref=src, dst_ref=dst, send_sem=s.at[i], recv_sem=r.at[i],
            device_id=to, device_id_type=pl.DeviceIdType.MESH,
        )

    copies = {}
    kinds = (
        ("route", routes, route_send, route_recv),
        ("tok", gathered, tok_send, tok_recv),
    )
    for name, buf, s, r in kinds:
        copies[name, n_z] = remote(buf.at[0], buf.at[n_z], s, r, n_z, x_peer)
        copies[name, n_z].start()
        for k in range(1, n_z):
            copies[name, k] = remote(buf.at[0], buf.at[k], s, r, k, z_peers[k - 1])
            copies[name, k].start()

    def place(p):
        block = gathered.at[p]
        pick, weighted = block_tables(routes[p], first_expert, count, top)
        picks[p] = pick.astype(BF16)
        weights[p] = weighted.astype(BF16)
        row_gate = jnp.sum(weighted, axis=1, keepdims=True)
        sel = pick.astype(BF16)
        at = slice(position[p] * CAP, (position[p] + 1) * CAP)
        a = jnp.dot(sel, block[:, :width], preferred_element_type=F32).astype(BF16)
        d = jnp.dot(sel, block[:, width:], preferred_element_type=F32) * row_gate
        d = d.astype(BF16)
        for e in range(count):
            rows_in[e, at, :] = a[e * CAP : (e + 1) * CAP]
            rows_dy[e, at, :] = d[e * CAP : (e + 1) * CAP]

    def arrived(p):
        copies["route", p].wait_recv()
        copies["tok", p].wait_recv()

    def column():
        for k in range(1, n_z):
            arrived(k)
            for name, buf, s, r in kinds:
                c = remote(buf.at[k], buf.at[n_z + k], s, r, n_z + k, x_peer)
                copies[name, n_z + k] = c
                c.start()
            place(k)

    def other_column():
        for k in range(1, n_z):
            arrived(n_z + k)
            place(n_z + k)

    keeps = []

    def keep(src, dst):
        keeps.append(pltpu.make_async_copy(src, dst, keep_sem.at[len(keeps)]))
        keeps[-1].start()

    def part(kind, e, at, dst):
        def tile(i, _):
            cols = pl.ds(pl.multiple_of(i * TILE, TILE), TILE)
            if kind == 2:
                v = lax.dot_general(
                    rows_dy[e, at, :], wd[e, cols, :], (((1,), (1,)), ((), ())),
                    preferred_element_type=F32,
                )
            else:
                w = wg if kind == 0 else wu
                v = jnp.dot(rows_in[e, at, :], w[e, :, cols], preferred_element_type=F32)
            dst[at, cols] = v.astype(BF16)
            return 0

        lax.fori_loop(0, ffw // TILE, tile, 0)

    step = 32
    core_copies, y_copies, loaded = {}, {}, set()

    def send_part(chunk):
        g, kind, j = chunk
        if kind not in loaded:
            loads[kind].wait()
            loaded.add(kind)
        i = kind * pairs + j
        part(kind, 2 * j + 1 - core, spans[g], away.at[i])
        c = remote(
            away.at[i, spans[g]], near.at[i, spans[g]], core_send, core_recv,
            g * 3 * pairs + i, core_peer,
        )
        core_copies[chunk] = c
        c.start()

    def each(g, f):
        def some(r, _):
            f(pl.ds(pl.multiple_of(spans[g].start + r * step, step), step))
            return 0

        lax.fori_loop(0, (spans[g].stop - spans[g].start) // step, some, 0)

    def send_sum(chunk):
        g, kind, j = chunk
        i = kind * pairs + j
        core_copies[chunk].wait_recv()

        def add(at):
            v = own[i, at, :].astype(F32) + near[i, at, :].astype(F32)
            own[i, at, :] = v.astype(BF16)

        each(g, add)
        c = remote(
            own.at[i, spans[g]], far.at[i, spans[g]], y_send, y_recv,
            g * 3 * pairs + i, y_peer,
        )
        y_copies[chunk] = c
        c.start()

    def run(chunks):
        for i, chunk in enumerate(chunks):
            g, kind, j = chunk
            send_part(chunk)
            if i > 0:
                send_sum(chunks[i - 1])
            part(kind, 2 * j + core, spans[g], own.at[kind * pairs + j])
        send_sum(chunks[-1])

    shares = {}

    def share(buf, e, g, i):
        c = remote(
            buf.at[e, spans[g]], buf.at[e, spans[g]], share_send, share_recv,
            g * 3 * pairs + i, core_peer,
        )
        shares[g, i] = c
        c.start()

    def total(kind, j, at):
        i = kind * pairs + j
        return own[i, at, :].astype(F32) + far[i, at, :].astype(F32)

    def forward(g):
        for j in range(pairs):
            e = 2 * j + core
            y_copies[g, 0, j].wait_recv()
            y_copies[g, 1, j].wait_recv()

            def some(at):
                v = total(0, j, at)
                hidden[e, at, :] = (v * jax.nn.sigmoid(v) * total(1, j, at)).astype(BF16)

            each(g, some)
            share(hidden, e, g, j)

    def backward(g):
        for j in range(pairs):
            e = 2 * j + core
            y_copies[g, 2, j].wait_recv()

            def some(at):
                v, u, h = total(0, j, at), total(1, j, at), total(2, j, at)
                s = jax.nn.sigmoid(v)
                up_grad[e, at, :] = (h * v * s).astype(BF16)
                gate_grad[e, at, :] = (h * u * s * (1.0 + v * (1.0 - s))).astype(BF16)

            each(g, some)
            share(gate_grad, e, g, pairs + j)
            share(up_grad, e, g, 2 * pairs + j)

    col_tiles = [(c, min(c + TILE, width)) for c in range(0, width, TILE)]

    def row_grads(at):
        def one(e, _):
            for a, b in col_tiles:
                dims = (((1,), (1,)), ((), ()))
                v = lax.dot_general(
                    gate_grad[e, at, :], wg[e, a:b, :], dims, preferred_element_type=F32
                ) + lax.dot_general(
                    up_grad[e, at, :], wu[e, a:b, :], dims, preferred_element_type=F32
                )
                results[e, at, a:b] = v.astype(BF16)
            return 0

        lax.fori_loop(0, count, one, 0)

    def to_tokens(tables, out, slots):
        for p in slots:
            at = slice(position[p] * CAP, (position[p] + 1) * CAP)
            rows = jnp.concatenate([results[e, at, :] for e in range(count)], axis=0)
            v = lax.dot_general(
                tables[p], rows, (((0,), (0,)), ((), ())), preferred_element_type=F32
            )
            out[p] = v.astype(BF16)

    place(0)
    arrived(n_z)
    place(n_z)
    every = range(pairs)
    run([(0, kind, j) for j in every for kind in (0, 1)] + [(0, 2, j) for j in every])
    column()
    run([(1, kind, j) for j in every for kind in (0, 1)])
    other_column()
    keep(rows_in, rows_in_out)
    keep(rows_dy, rows_dy_out)
    run(
        [(2, kind, j) for j in every for kind in (0, 1)]
        + [(2, 2, j) for j in every]
        + [(1, 2, j) for j in every]
    )
    forward(0)
    backward(0)
    forward(1)
    forward(2)
    for g in range(3):
        for j in every:
            shares[g, j].wait_recv()
    keep(hidden, hidden_out)

    def out_rows(e, _):
        for a, b in col_tiles:
            v = jnp.dot(hidden[e], wd[e, :, a:b], preferred_element_type=F32)
            results[e, :, a:b] = v.astype(BF16)
        return 0

    lax.fori_loop(0, count, out_rows, 0)
    to_tokens(weights, partial, range(n_ex))
    across = remote(partial.at[n_z:], from_x, ret_send, ret_recv, 0, x_peer)
    across.start()
    backward(2)
    for g in (0, 2):
        for i in range(pairs, 3 * pairs):
            shares[g, i].wait_recv()
    row_grads(slice(0, spans[2].stop))
    to_tokens(picks, token_partial, range(n_z, n_ex))
    token_across = remote(token_partial.at[n_z:], token_x, ret_send, ret_recv, n_z, x_peer)
    token_across.start()

    def add_x(mine, other):
        for k in range(n_z):
            mine[k] = (mine[k].astype(F32) + other[k].astype(F32)).astype(BF16)

    across.wait_recv()
    add_x(partial, from_x)
    along = []
    for k in range(1, n_z):
        along.append(
            remote(
                partial.at[k], from_z.at[k - 1], ret_send, ret_recv, k, z_peers[n_z - k - 1]
            )
        )
        along[-1].start()
    backward(1)
    for i in range(pairs, 3 * pairs):
        shares[1, i].wait_recv()
    keep(gate_grad, gate_grad_out)
    keep(up_grad, up_grad_out)
    row_grads(spans[1])
    to_tokens(picks, token_partial, range(n_z))
    token_across.wait_recv()
    add_x(token_partial, token_x)
    keep(token_partial.at[:n_z], token_out)
    v = partial[0].astype(F32)
    for k, c in enumerate(along):
        c.wait_recv()
        v += from_z[k].astype(F32)
    mixed_ref[...] = v.astype(BF16)

    for group in (copies, core_copies, y_copies, shares):
        for c in group.values():
            c.wait_send()
    for c in [across, token_across] + along:
        c.wait_send()
    for c in keeps:
        c.wait()


def front(tokens, cotangent, ids, gates, w_gate, w_up, w_down, n_ex):
    count, width, ffw = w_gate.shape
    rows = n_ex * CAP
    tok = tokens.shape[0]
    pairs = count // 2
    n_z = n_ex // 2
    shape = jax.ShapeDtypeStruct
    vmem = pl.BlockSpec(memory_space=pltpu.VMEM)
    hbm = pl.BlockSpec(memory_space=pl.ANY)
    dma = pltpu.SemaphoreType.DMA
    return pl.pallas_call(
        front_kernel,
        out_shape=[
            shape((tok, width), BF16),
            shape((n_z, tok, width), BF16),
            shape((count, rows, width), BF16),
            shape((count, rows, width), BF16),
            shape((count, rows, ffw), BF16),
            shape((count, rows, ffw), BF16),
            shape((count, rows, ffw), BF16),
        ],
        in_specs=[vmem] * 4 + [hbm] * 3,
        out_specs=[vmem] + [hbm] * 6,
        scratch_shapes=[
            pltpu.VMEM(w_gate.shape, BF16),
            pltpu.VMEM(w_up.shape, BF16),
            pltpu.VMEM(w_down.shape, BF16),
            pltpu.VMEM((n_ex, tok, 2 * width), BF16),
            pltpu.VMEM((n_ex, 2 * ids.shape[0], tok), F32),
            pltpu.VMEM((count, rows, width), BF16),
            pltpu.VMEM((count, rows, width), BF16),
            pltpu.VMEM((n_ex, count * CAP, tok), BF16),
            pltpu.VMEM((n_ex, count * CAP, tok), BF16),
        ]
        + [pltpu.VMEM((3 * pairs, rows, ffw), BF16)] * 4
        + [pltpu.VMEM((count, rows, ffw), BF16)] * 3
        + [pltpu.VMEM((count, rows, width), BF16)]
        + [pltpu.VMEM((n_ex, tok, width), BF16)] * 2
        + [pltpu.VMEM((n_z, tok, width), BF16), pltpu.VMEM((n_z - 1, tok, width), BF16)]
        + [pltpu.VMEM((n_z, tok, width), BF16)]
        + [dma((3,)), dma((6,))]
        + [dma((n_ex,))] * 4
        + [dma((9 * pairs,))] * 6
        + [dma((n_z + 1,))] * 2,
        compiler_params=pltpu.CompilerParams(
            collective_id=0, has_side_effects=True, vmem_limit_bytes=60 * 1024 * 1024
        ),
        cost_estimate=pl.CostEstimate(
            flops=12 * count * rows * width * ffw, bytes_accessed=64 << 20, transcendentals=0
        ),
        name="front",
    )(tokens, cotangent, ids, gates, w_gate, w_up, w_down)


def front_general(both, route, w_gate, w_up, w_down, n_ex):
    count, width, _ = w_gate.shape
    rows = n_ex * CAP
    top = route.shape[1] // 2
    route = lax.all_gather(route, "expert", axis=0, tiled=True)
    both = lax.all_gather(both, "expert", axis=0, tiled=True)
    pick, weighted, row_gate = tables(
        route[:, :top].astype(jnp.int32),
        route[:, top:],
        lax.axis_index("expert") * count,
        count,
        n_ex,
    )
    picked = mm(pick, both)
    rows_in = picked[:, :width].astype(BF16).reshape(count, rows, width)
    rows_dy = (picked[:, width:] * row_gate).astype(BF16).reshape(count, rows, width)

    def gate_up(e, w):
        return mm(rows_in[e], w[e]).astype(BF16)

    def back(e):
        return mm(rows_dy[e], w_down[e], ((1,), (1,))).astype(BF16)

    def forward(gate_sum, up_sum):
        logistic = jax.nn.sigmoid(gate_sum)
        return (gate_sum * logistic * up_sum).astype(BF16)

    def backward(gate_sum, up_sum, hidden_grad):
        logistic = jax.nn.sigmoid(gate_sum)
        up_grad = (hidden_grad * gate_sum * logistic).astype(BF16)
        gate_grad = (
            hidden_grad * up_sum * logistic * (1.0 + gate_sum * (1.0 - logistic))
        ).astype(BF16)
        return gate_grad, up_grad

    gate_sum, up_sum, hidden_grad = (
        lax.psum(jnp.stack(p), "dp").astype(F32)
        for p in (
            [gate_up(e, w_gate) for e in range(count)],
            [gate_up(e, w_up) for e in range(count)],
            [back(e) for e in range(count)],
        )
    )
    hidden = forward(gate_sum, up_sum)
    gate_grad, up_grad = backward(gate_sum, up_sum, hidden_grad)

    return rows_in, rows_dy, pick, weighted, hidden, gate_grad, up_grad


def weight_grad(a, b):
    return jnp.einsum("erm,ern->emn", a, b, preferred_element_type=F32).astype(BF16)


def weights_kernel(x_ref, dy_ref, gate_ref, up_ref, hidden_ref, gate_out, up_out, down_out, xt):
    width = x_ref.shape[2]
    part = gate_ref.shape[2]

    @pl.when(pl.program_id(1) == 0)
    def _():
        xt[...] = x_ref[0].T

    for ref, out in ((gate_ref, gate_out), (up_ref, up_out)):
        for c in range(0, part, TILE):
            at = slice(c, c + TILE)
            v = jnp.dot(xt[...], ref[0, :, at], preferred_element_type=F32)
            out[0, :, at] = v.astype(BF16)
    ht = hidden_ref[0].T
    for c in range(0, width, TILE):
        at = slice(c, min(c + TILE, width))
        v = jnp.dot(ht, dy_ref[0, :, at], preferred_element_type=F32)
        down_out[0, :, at] = v.astype(BF16)


def weight_grads(rows_in, rows_dy, gate_grad, up_grad, hidden):
    count, rows, width = rows_in.shape
    ffw = hidden.shape[2]
    part = ffw // 2
    wide = pl.BlockSpec((1, rows, width), lambda e, n: (e, 0, 0))
    some = pl.BlockSpec((1, rows, part), lambda e, n: (e, 0, n))
    out = pl.BlockSpec((1, width, part), lambda e, n: (e, 0, n))
    down = pl.BlockSpec((1, part, width), lambda e, n: (e, n, 0))
    shape = jax.ShapeDtypeStruct
    return pl.pallas_call(
        weights_kernel,
        grid=(count, 2),
        out_shape=[
            shape((count, width, ffw), BF16),
            shape((count, width, ffw), BF16),
            shape((count, ffw, width), BF16),
        ],
        in_specs=[wide, wide, some, some, some],
        out_specs=[out, out, down],
        scratch_shapes=[pltpu.VMEM((width, rows), BF16)],
        compiler_params=pltpu.CompilerParams(vmem_limit_bytes=60 * 1024 * 1024),
        cost_estimate=pl.CostEstimate(
            flops=6 * count * rows * width * ffw, bytes_accessed=32 << 20, transcendentals=0
        ),
        name="weight_grads",
    )(rows_in, rows_dy, gate_grad, up_grad, hidden)


def make_body(n_dp, n_ex):
    fast = n_dp == 4 and n_ex == 8

    def body(tokens, expert_ids, gate_weights, w_gate, w_up, w_down, cotangent):
        count = w_gate.shape[0]
        if fast:
            mixed, col, rows_in, rows_dy, hidden, gate_grad, up_grad = front(
                tokens, cotangent, expert_ids.T, gate_weights.T, w_gate, w_up, w_down, n_ex
            )
            token_grad = add_along(col, n_ex)
            grad_gate, grad_up, grad_down = weight_grads(
                rows_in, rows_dy, gate_grad, up_grad, hidden
            )
        else:
            both = jnp.concatenate([tokens, cotangent], axis=1)
            route = jnp.concatenate([expert_ids.astype(F32), gate_weights], axis=1)
            rows_in, rows_dy, pick, weighted, hidden, gate_grad, up_grad = front_general(
                both, route, w_gate, w_up, w_down, n_ex
            )
            out_rows = [mm(hidden[e], w_down[e]).astype(BF16) for e in range(count)]
            row_grad = [
                (
                    mm(gate_grad[e], w_gate[e], ((1,), (1,))) + mm(up_grad[e], w_up[e], ((1,), (1,)))
                ).astype(BF16)
                for e in range(count)
            ]
            mixed = mm(weighted, jnp.concatenate(out_rows), ((0,), (0,))).astype(BF16)
            token_grad = mm(pick, jnp.concatenate(row_grad), ((0,), (0,))).astype(BF16)
            mixed, token_grad = (
                lax.psum_scatter(v, "expert", scatter_dimension=0, tiled=True)
                for v in (mixed, token_grad)
            )
            grad_down = weight_grad(hidden, rows_dy)
            grad_gate = weight_grad(rows_in, gate_grad)
            grad_up = weight_grad(rows_in, up_grad)
        return mixed, token_grad, grad_gate, grad_up, grad_down

    return body


def solution(mesh):
    placed = (
        P("expert", "dp"),
        P("expert", None),
        P("expert", None),
        P("expert", "dp", None),
        P("expert", "dp", None),
        P("expert", None, "dp"),
        P("expert", "dp"),
    )
    return jax.shard_map(
        make_body(mesh.shape["dp"], mesh.shape["expert"]),
        mesh=mesh,
        in_specs=placed,
        out_specs=(
            P("expert", "dp"),
            P("expert", "dp"),
            P("expert", "dp", None),
            P("expert", "dp", None),
            P("expert", None, "dp"),
        ),
        check_vma=False,
    )
```
